32 devices in a mesh: grp: 2 (over y), band: 4 (over z), sect: 4 (over x, core).
Axes of the slice: x: 2, y: 2, z: 4, core: 2. Of those that a mesh axis runs over, the one named last changes fastest.
Arguments:
- features: bfloat16 [4, 24, 96, 2048], P('grp', 'band', None, 'sect'), parts along dimension 0, may hold values from -16 to 16
- low_level: bfloat16 [4, 24, 96, 256], P('grp', 'band'), parts along dimension 0, may hold values from -6 to 6
- land_mask: int32 [4, 24], P('grp', 'band'), parts along dimension 0, may hold values from 0 to 1, as said below
- weight_one: bfloat16 [2048, 256], P('sect'), may hold values from -0.125 to 0.125
- weight_dilated: bfloat16 [3, 3, 3, 2048, 256], P(None, None, None, 'sect'), may hold values from -0.046875 to 0.046875
- bias_branch: float32 [4, 256], replicated, may hold values from -3 to 3
- weight_pool: bfloat16 [2048, 256], P('sect'), may hold values from -0.125 to 0.125
- bias_pool: float32 [256], replicated, may hold values from -3 to 3
- weight_project: bfloat16 [1280, 256], replicated, may hold values from -0.15625 to 0.15625
- bias_project: float32 [256], replicated, may hold values from -3 to 3
- weight_reduce: bfloat16 [256, 48], replicated, may hold values from -0.375 to 0.375
- bias_reduce: float32 [48], replicated, may hold values from -3 to 3
- weight_merging: bfloat16 [3, 3, 304, 256], replicated, may hold values from -0.109375 to 0.109375
- bias_merging: float32 [256], replicated, may hold values from -3 to 3
Outputs:
- merged_map: bfloat16 [4, 24, 96, 256], P('grp', 'band'), parts along dimension 0
The draws below stay inside these ranges and needn't reach their ends.
There are 2 independent parts, one for each index of `grp`. The reference program is written for one: setup_inputs(seed, part) draws one part's arguments, and reference() takes and returns one part's arrays. A program takes and returns all parts, laid end to end along the dimension named above; an argument that names none is the same for every part. Nothing has to cross between parts.
Inputs may be any that keep to these rules, and one draw needn't show every extreme that they name: `land_mask`: in every image each aligned block of 6 rows holds at most 4 ones and at least 2 ones, its first and last rows always being ones; in every image some block holds exactly 4.
All inputs are finite; a program needn't handle non-finite values.
Results may differ from the reference program's by a relative error of at most 0.012.
Values may be sent and summed in bfloat16 or wider, within the bound.
No kernel may reach another device: no remote copies, remote signals or barrier semaphores. Data moves between devices by JAX's collectives and lax.ppermute only.
A program may use at most 64 MiB of HBM per device.

```python
import jax
import jax.numpy as jnp
from jax import lax

C = 2048
BR = 256
LOW = 256
LOWP = 48
DEC = 256
W = 96
MB = 2
R_DEV = 6
ACT_DEV = 4
H = 24
N_SECT = 4


def draw_features(key, part):
    base = jax.random.fold_in(key, 11)
    key_noise, key_mean, key_rows = jax.random.split(base, 3)
    rough = jax.random.normal(key_noise, (MB, H, W, C), jnp.float32)
    channel_mean = jax.random.normal(key_mean, (C,), jnp.float32) * 0.7
    row_ramp = 1.0 + 2.0 * jnp.arange(H, dtype=jnp.float32) / H
    row_factor = row_ramp[None, :] * jax.random.uniform(key_rows, (MB, H), jnp.float32, 0.5, 1.5)
    values = rough + channel_mean[None, None, None, :] * row_factor[:, :, None, None]
    return jnp.clip(values, -16.0, 16.0).astype(jnp.bfloat16)


def draw_land_mask(key, part):
    base = jax.random.fold_in(key, 7)
    key_count, key_full, key_order = jax.random.split(base, 3)
    band_count = H // R_DEV
    counts = jax.random.randint(key_count, (MB, band_count), ACT_DEV - ACT_DEV // 2, ACT_DEV + 1)
    full_band = jax.random.randint(key_full, (MB, 1), 0, band_count)
    counts = jnp.where(jnp.arange(band_count)[None, :] == full_band, ACT_DEV, counts)
    row_index = jnp.arange(R_DEV, dtype=jnp.int32)
    edge_row = (row_index == 0) | (row_index == R_DEV - 1)
    random_part = (jax.random.randint(key_order, (MB, band_count, R_DEV), 0, 2 ** 20) + 1) * R_DEV + row_index[None, None, :]
    scores = jnp.where(edge_row[None, None, :], row_index[None, None, :], random_part)
    rank_of = jnp.argsort(jnp.argsort(scores, axis=2), axis=2)
    land_rows = (rank_of < counts[:, :, None]).astype(jnp.int32)
    return land_rows.reshape(MB, H)


def shard_levels(key, shape, cuts, smallest, top_value):
    def one(position, parts):
        heights = jax.random.uniform(jax.random.fold_in(jax.random.fold_in(key, 6), position), (parts,), jnp.float32, smallest / len(cuts), top_value / len(cuts))
        return jnp.repeat(jnp.exp(heights), shape[position] // parts).reshape((-1,) + (1,) * (len(shape) - position - 1))

    gain = one(*cuts[0])
    for cut in cuts[1:]:
        gain = gain * one(*cut)
    return gain


def gaussian(own_key, shape, width, limit, cuts=(), held_as=jnp.bfloat16):
    array = width * jax.random.normal(own_key, shape, jnp.float32)
    if cuts:
        array = array * shard_levels(own_key, shape, cuts, -0.22, 0.18)
    return jnp.clip(array, -limit, limit).astype(held_as)


def setup_inputs(seed: int = 0, part: int = 0) -> dict:
    key_list = jax.random.split(jax.random.key(seed), 15)
    part_keys = jax.random.split(jax.random.fold_in(key_list[14], part), 15)
    return {
        "features": draw_features(jax.random.fold_in(jax.random.fold_in(key_list[14], part), 71), part),
        "low_level": gaussian(part_keys[1], (MB, H, W, LOW), 1.0, 6.0, ((1, 4),)),
        "land_mask": draw_land_mask(jax.random.fold_in(jax.random.fold_in(key_list[14], part), 71), part),
        "weight_one": gaussian(key_list[3], (C, BR), C ** -0.5, 0.125, ((0, 4),)),
        "weight_dilated": gaussian(key_list[4], (3, 3, 3, C, BR), (9 * C) ** -0.5, 0.046875, ((3, 4),)),
        "bias_branch": gaussian(key_list[5], (4, BR), 0.5, 3.0, (), jnp.float32),
        "weight_pool": gaussian(key_list[6], (C, BR), C ** -0.5, 0.125, ((0, 4),)),
        "bias_pool": gaussian(key_list[7], (BR,), 0.5, 3.0, (), jnp.float32),
        "weight_project": gaussian(key_list[8], (5 * BR, BR), (5 * BR) ** -0.5, 0.15625),
        "bias_project": gaussian(key_list[9], (BR,), 0.5, 3.0, (), jnp.float32),
        "weight_reduce": gaussian(key_list[10], (LOW, LOWP), LOW ** -0.5, 0.375),
        "bias_reduce": gaussian(key_list[11], (LOWP,), 0.5, 3.0, (), jnp.float32),
        "weight_merging": gaussian(key_list[12], (3, 3, BR + LOWP, DEC), (9 * (BR + LOWP)) ** -0.5, 0.109375),
        "bias_merging": gaussian(key_list[13], (DEC,), 0.5, 3.0, (), jnp.float32),
    }


DILATIONS = (12, 24, 36)
PADDING = 36
PRECISE = lax.Precision.HIGHEST


def group_partial(sample_map, weight_one, weight_dilated, first_channel, group_width):
    height, breadth = sample_map.shape[0], sample_map.shape[1]
    section = sample_map[:, :, first_channel:first_channel + group_width]
    padded = jnp.pad(section, ((PADDING, PADDING), (PADDING, PADDING), (0, 0)))
    partials = [jnp.dot(section.reshape(-1, group_width), weight_one[first_channel:first_channel + group_width], preferred_element_type=jnp.float32)]
    for branch_index, dilation in enumerate(DILATIONS):
        running = jnp.zeros((height * breadth, weight_one.shape[1]), jnp.float32)
        for row_tap in range(3):
            for col_tap in range(3):
                top = PADDING + dilation * (row_tap - 1)
                left = PADDING + dilation * (col_tap - 1)
                tap_rows = padded[top:top + height, left:left + breadth].reshape(-1, group_width)
                running = running + jnp.dot(tap_rows, weight_dilated[branch_index, row_tap, col_tap, first_channel:first_channel + group_width], preferred_element_type=jnp.float32)
        partials.append(running)
    return jnp.concatenate(partials, axis=1).astype(jnp.bfloat16)


def reference(features, low_level, land_mask, weight_one, weight_dilated, bias_branch, weight_pool, bias_pool, weight_project, bias_project, weight_reduce, bias_reduce, weight_merging, bias_merging):
    group_width = C // N_SECT
    results = []
    for sample in range(MB):
        sample_map = features[sample]
        pre_branch = jnp.zeros((H * W, 4 * BR), jnp.float32)
        for group_index in range(N_SECT):
            pre_branch = pre_branch + group_partial(sample_map, weight_one, weight_dilated, group_index * group_width, group_width).astype(jnp.float32)
        branch = jax.nn.relu(pre_branch + bias_branch.reshape(-1)).astype(jnp.bfloat16)
        average = jnp.sum(sample_map, axis=(0, 1), dtype=jnp.float32) / (H * W)
        pooled = jax.nn.relu(jnp.dot(average, weight_pool.astype(jnp.float32), precision=PRECISE) + bias_pool)
        context = jnp.dot(pooled, weight_project[4 * BR:].astype(jnp.float32), precision=PRECISE)
        row_keep = land_mask[sample].astype(jnp.float32)
        projected = jnp.dot(branch, weight_project[:4 * BR], preferred_element_type=jnp.float32) + context + bias_project
        project_out = (jax.nn.relu(projected).reshape(H, W, BR) * row_keep[:, None, None]).astype(jnp.bfloat16)
        low_reduced = jax.nn.relu(jnp.dot(low_level[sample].reshape(-1, LOW), weight_reduce, preferred_element_type=jnp.float32) + bias_reduce).astype(jnp.bfloat16).reshape(H, W, LOWP)
        joined = jnp.concatenate([project_out, low_reduced], axis=2)
        framed = jnp.pad(joined, ((1, 1), (1, 1), (0, 0)))
        running = jnp.zeros((H * W, DEC), jnp.float32)
        for row_tap in range(3):
            for col_tap in range(3):
                running = running + jnp.dot(framed[row_tap:row_tap + H, col_tap:col_tap + W].reshape(-1, BR + LOWP), weight_merging[row_tap, col_tap], preferred_element_type=jnp.float32)
        merged_map = (jax.nn.relu(running + bias_merging).reshape(H, W, DEC) * row_keep[:, None, None]).astype(jnp.bfloat16)
        results.append(merged_map)
    return jnp.stack(results)
```

```python
import functools

import jax
import jax.numpy as jnp
from jax import lax
from jax.experimental import pallas as pl
from jax.experimental.pallas import tpu as pltpu
from jax.sharding import PartitionSpec as P

DILATIONS = (12, 24, 36)
PADDING = 36
PRECISE = lax.Precision.HIGHEST
ROW_BLOCK = 6
MOST_LAND = 4
VMEM_LIMIT = 50 * 2 ** 20
F32 = jnp.float32
BF16 = jnp.bfloat16
VMEM = pl.BlockSpec(memory_space=pltpu.VMEM)
SMEM = pl.BlockSpec(memory_space=pltpu.SMEM)
ANY = pl.BlockSpec(memory_space=pl.ANY)


def call(body, outs, in_specs, scratch, flops, bytes_accessed):
    return pl.pallas_call(
        body,
        out_shape=outs,
        in_specs=in_specs,
        out_specs=jax.tree.map(lambda _: VMEM, outs),
        scratch_shapes=scratch,
        compiler_params=pltpu.CompilerParams(vmem_limit_bytes=VMEM_LIMIT),
        cost_estimate=pl.CostEstimate(
            flops=flops, bytes_accessed=bytes_accessed, transcendentals=0
        ),
    )


def reversed_bits(value, bits):
    return sum(((value >> bit) & 1) << (bits - 1 - bit) for bit in range(bits))


def fill_slots(mask_ref, slots_ref, batches, row_count):
    for image in range(batches):
        inner = range(1, row_count - 1)
        lives = {row: (mask_ref[image, row] > 0).astype(jnp.int32) for row in inner}
        land_total = sum(lives.values())
        land_before, sea_before = 0, 0
        chosen = [0] * (MOST_LAND - 2)
        for row in inner:
            live = lives[row]
            rank = jnp.where(live > 0, land_before, land_total + sea_before)
            chosen = [
                value + row * (rank == slot).astype(jnp.int32)
                for slot, value in enumerate(chosen)
            ]
            land_before = land_before + live
            sea_before = sea_before + (1 - live)
        base = image * MOST_LAND
        slots_ref[base] = jnp.int32(0)
        for slot, value in enumerate(chosen):
            slots_ref[base + 1 + slot] = value
        slots_ref[base + MOST_LAND - 1] = jnp.int32(row_count - 1)


def split_three(value):
    high = value.astype(BF16)
    rest = value - high.astype(F32)
    middle = rest.astype(BF16)
    low = (rest - middle.astype(F32)).astype(BF16)
    return high, middle, low


def precise_dot(value, weight):
    return sum(jnp.dot(part, weight, preferred_element_type=F32) for part in split_three(value))


def shifted(value, by, columns):
    column = lax.broadcasted_iota(jnp.int32, value.shape, 0) % columns
    moved = pltpu.roll(value, by % value.shape[0], 0)
    inside = column >= by if by > 0 else column < columns + by
    return jnp.where(inside, moved, 0.0)


class Plan:
    def __init__(self, batches, row_count, columns, bands, sects):
        self.batches, self.row_count, self.columns = batches, row_count, columns
        self.bands, self.sects = bands, sects
        self.bits = sects.bit_length() - 1
        self.share_rows = batches * MOST_LAND // sects
        self.share = self.share_rows * columns
        self.terms = []
        for branch, dilation in enumerate(DILATIONS):
            hop = dilation // row_count
            if hop >= bands:
                continue
            up = [(b, b + hop) for b in range(bands - hop)]
            down = [(target, source) for source, target in up]
            if 2 * hop >= bands:
                self.terms.append((branch, hop, None, up + down))
            else:
                self.terms.append((branch, hop, 0, up))
                self.terms.append((branch, hop, 2, down))

    def tap_columns(self, dilation):
        return [1] + ([0, 2] if dilation < self.columns else [])


def branch_kernel(plan, place_ref, mask_ref, far_mask_ref, features_ref, one_ref, dilated_ref, *refs):
    terms = len(plan.terms)
    outs = refs[: 2 + (2 if terms else 0)]
    slots_ref, rows_ref, weights_ref, row_sems, weight_sems = refs[len(outs) :]
    columns, width = plan.columns, one_ref.shape[1]
    half = plan.sects // 2 * plan.share
    sect, band = place_ref[0], place_ref[1]

    def fetch_rows(group, mask):
        fill_slots(mask, slots_ref, plan.batches, plan.row_count)
        copies = []
        for position in range(plan.sects):
            owner = sect ^ reversed_bits(position, plan.bits)
            for row in range(plan.share_rows):
                place = owner * plan.share_rows + row
                image = lax.div(place, MOST_LAND)
                index = position * plan.share_rows + row
                copies.append(
                    pltpu.make_async_copy(
                        features_ref.at[image, slots_ref[place]],
                        rows_ref.at[group, pl.ds(index * columns, columns)],
                        row_sems.at[group, index],
                    )
                )
                copies[-1].start()
        return copies

    weight_copies = []

    def fetch_weight(source):
        index = len(weight_copies)
        copy = pltpu.make_async_copy(source, weights_ref.at[index], weight_sems.at[index])
        copy.start()
        weight_copies.append(copy)

    def product(group, index):
        weight_copies[index].wait()
        return jnp.dot(rows_ref[group], weights_ref[index], preferred_element_type=F32)

    own_rows = fetch_rows(0, mask_ref)
    fetch_weight(one_ref)
    work = [(0, 0, None, [(0, 0)])]
    for branch, dilation in enumerate(DILATIONS):
        taps = []
        for tap in plan.tap_columns(dilation):
            taps.append((len(weight_copies), (1 - tap) * dilation))
            fetch_weight(dilated_ref.at[branch, 1, tap])
        work.append((0, branch + 1, None, taps))
    term_rows = []
    for term, (branch, hop, row_tap, _) in enumerate(plan.terms):
        term_rows.append(fetch_rows(term + 1, far_mask_ref.at[term]))
        if row_tap is None:
            row_tap = jnp.where(band + hop < plan.bands, 0, 2)
        taps = []
        for tap in plan.tap_columns(DILATIONS[branch]):
            taps.append((len(weight_copies), (1 - tap) * DILATIONS[branch]))
            fetch_weight(dilated_ref.at[branch, row_tap, tap])
        work.append((term + 1, None, term, taps))
    for copy in own_rows:
        copy.wait()
    for group, branch, term, taps in work:
        if term is not None:
            for copy in term_rows[term]:
                copy.wait()
        total = product(group, taps[0][0])
        for index, by in taps[1:]:
            total = total + shifted(product(group, index), by, columns)
        total = total.astype(BF16)
        keep, send = outs[:2] if term is None else outs[2:]
        place = branch if term is None else term
        keep[:, pl.ds(place * width, width)] = total[:half]
        send[:, pl.ds(place * width, width)] = total[half:]


def branch_partials(plan, place, mask, far_mask, features, weight_one, weight_dilated):
    terms = len(plan.terms)
    channels, width = weight_one.shape
    half = plan.sects // 2 * plan.share
    own = jax.ShapeDtypeStruct((half, 4 * width), BF16)
    outs = [own, own]
    if terms:
        far = jax.ShapeDtypeStruct((half, terms * width), BF16)
        outs += [far, far]
    weights = 1 + 9 + 3 * terms
    scratch = [
        pltpu.SMEM((plan.batches * MOST_LAND,), jnp.int32),
        pltpu.VMEM((1 + terms, 2 * half, channels), BF16),
        pltpu.VMEM((weights, channels, width), BF16),
        pltpu.SemaphoreType.DMA((1 + terms, plan.batches * MOST_LAND)),
        pltpu.SemaphoreType.DMA((weights,)),
    ]
    flops = 2 * weights * 2 * half * channels * width
    return call(
        functools.partial(branch_kernel, plan),
        tuple(outs),
        [SMEM, SMEM, SMEM, ANY, ANY, ANY],
        scratch,
        flops,
        2 * (weights * channels * width + (1 + terms) * 2 * half * channels),
    )(place, mask, far_mask, features, weight_one, weight_dilated)


def pool_kernel(features_ref, weight_ref, out_ref):
    batches, row_count, columns, channels = features_ref.shape
    sums = [
        jnp.sum(
            features_ref[image].astype(F32).reshape(row_count * columns, channels),
            axis=0,
            keepdims=True,
        )
        for image in range(batches)
    ]
    row = lax.broadcasted_iota(jnp.int32, (out_ref.shape[0], channels), 0)
    stacked = jnp.zeros((out_ref.shape[0], channels), F32)
    for image, value in enumerate(sums):
        stacked = jnp.where(row == image, value, stacked)
    out_ref[...] = precise_dot(stacked, weight_ref[...])


def low_kernel(place_ref, low_ref, first_ref, second_ref, reduce_ref, bias_reduce_ref, merging_ref, bias_ref, out_ref, framed_ref):
    batches, row_count, columns, depth = low_ref.shape
    band, bands = place_ref[1], place_ref[2]
    wide = reduce_ref.shape[1]
    reduced = wide // 3
    even = band % 2 == 0

    def reduce(rows):
        value = jnp.dot(rows, reduce_ref[...], preferred_element_type=F32) + bias_reduce_ref[...]
        value = jnp.maximum(value, 0.0).astype(BF16).astype(F32)
        lane = lax.broadcasted_iota(jnp.int32, value.shape, 1)
        return jnp.where(
            lane < reduced,
            shifted(value, 1, columns),
            jnp.where(lane < 2 * reduced, value, shifted(value, -1, columns)),
        )

    framed_ref[:, 1 : row_count + 1] = (
        reduce(low_ref[...].reshape(-1, depth)).astype(BF16).reshape(batches, row_count, columns, wide)
    )
    first = reduce(first_ref[...].reshape(-1, depth))
    second = reduce(second_ref[...].reshape(-1, depth))
    above = jnp.where(even, second, first) * jnp.where(band > 0, 1.0, 0.0)
    below = jnp.where(even, first, second) * jnp.where(band < bands - 1, 1.0, 0.0)
    framed_ref[:, 0] = above.astype(BF16).reshape(batches, columns, wide)
    framed_ref[:, row_count + 1] = below.astype(BF16).reshape(batches, columns, wide)
    for image in range(batches):
        total = jnp.zeros((row_count * columns, out_ref.shape[3]), F32) + bias_ref[...]
        for tap in range(3):
            rows = framed_ref[image, tap : tap + row_count].reshape(-1, wide)
            total = total + jnp.dot(rows, merging_ref[tap], preferred_element_type=F32)
        out_ref[image] = total.reshape(row_count, columns, -1)


def project_kernel(plan, place_ref, mask_ref, keep_ref, moved_ref, bias_branch_ref, pool_ref, bias_pool_ref, weight_ref, bias_ref, *refs):
    far_refs = refs[: len(plan.terms)]
    out_ref, edge_ref, slots_ref, context_ref = refs[len(plan.terms) :]
    columns, width = plan.columns, weight_ref.shape[1]
    sect = place_ref[0]
    fill_slots(mask_ref, slots_ref, plan.batches, plan.row_count)
    cells = plan.row_count * plan.bands * columns
    pooled = jnp.maximum(pool_ref[...] / cells + bias_pool_ref[...], 0.0)
    context_ref[...] = precise_dot(pooled, weight_ref[4 * width :]) + bias_ref[...]
    total = jnp.zeros((plan.share, width), F32)
    for branch in range(4):
        lanes = pl.ds(branch * width, width)
        value = keep_ref[:, lanes].astype(F32) + moved_ref[:, lanes].astype(F32)
        for term, far in zip(plan.terms, far_refs):
            if term[0] + 1 == branch:
                value = value + far[...].astype(F32)
        value = jnp.maximum(value + bias_branch_ref[pl.ds(branch, 1)], 0.0).astype(BF16)
        total = total + jnp.dot(
            value, weight_ref[pl.ds(branch * width, width)], preferred_element_type=F32
        )
    for row in range(plan.share_rows):
        place = sect * plan.share_rows + row
        image = lax.div(place, MOST_LAND)
        keep = mask_ref[image, slots_ref[place]].astype(F32)
        value = total[row * columns : (row + 1) * columns] + context_ref[pl.ds(image, 1)]
        out_ref[pl.ds(row * columns, columns)] = (jnp.maximum(value, 0.0) * keep).astype(BF16)
    at_top = lax.rem(sect * plan.share_rows, MOST_LAND) == 0

    @pl.when(at_top)
    def _():
        edge_ref[...] = out_ref[pl.ds(0, columns)]

    @pl.when(jnp.logical_not(at_top))
    def _():
        edge_ref[...] = out_ref[pl.ds(plan.share - columns, columns)]


def merge_kernel(plan, place_ref, mask_ref, low_ref, weight_ref, *refs):
    sects, columns = plan.sects, plan.columns
    share_refs, edge_refs = refs[:sects], refs[sects : 2 * sects]
    out_ref, slots_ref, rows_ref, halo_ref, total_ref = refs[2 * sects :]
    width = weight_ref.shape[3]
    sect = place_ref[0]
    fill_slots(mask_ref, slots_ref, plan.batches, plan.row_count)

    def spread(value):
        wide = value.astype(F32)
        return (
            shifted(wide, 1, columns).astype(BF16),
            value,
            shifted(wide, -1, columns).astype(BF16),
        )

    def weight(tap):
        return jnp.concatenate([weight_ref[tap, side, :width] for side in range(3)], axis=0)

    total_ref[:, 1 : plan.row_count + 1] = low_ref[...]
    tops, bottoms = [], []
    for offset in range(sects):
        for side, value in enumerate(spread(share_refs[offset][...])):
            rows_ref[pl.ds(offset * plan.share, plan.share), pl.ds(side * width, width)] = value
        for side, value in enumerate(spread(edge_refs[offset][...])):
            halo_ref[pl.ds(offset * columns, columns), pl.ds(side * width, width)] = value
    for tap in range(3):
        taps = weight(tap)
        result = jnp.dot(rows_ref[...], taps, preferred_element_type=F32)
        if tap != 1:
            halo = jnp.dot(halo_ref[...], taps, preferred_element_type=F32)
        for offset in range(sects):
            owner = sect ^ offset
            for row in range(plan.share_rows):
                place = owner * plan.share_rows + row
                image = lax.div(place, MOST_LAND)
                at = slots_ref[place] + 2 - tap
                start = (offset * plan.share_rows + row) * columns
                total_ref[image, at] = total_ref[image, at] + result[start : start + columns]
            first = owner * plan.share_rows
            image = lax.div(first, MOST_LAND)
            top = lax.rem(first, MOST_LAND) == 0
            bottom = lax.rem(first + plan.share_rows, MOST_LAND) == 0
            if tap != 1:
                piece = halo[offset * columns : (offset + 1) * columns]
                at = 1 if tap == 0 else plan.row_count
                factor = jnp.where(top if tap == 0 else bottom, 1.0, 0.0)
                total_ref[image, at] = total_ref[image, at] + piece * factor
    for image in range(plan.batches):
        for row in range(plan.row_count):
            keep = mask_ref[image, row].astype(F32)
            out_ref[image, row] = (jnp.maximum(total_ref[image, row + 1], 0.0) * keep).astype(BF16)


def swap(value, axis, pattern):
    count = lax.axis_size(axis)
    return lax.ppermute(value, axis, [(i, i ^ pattern) for i in range(count)])


def add_halves(keep, moved):
    total = (keep.astype(F32) + moved.astype(F32)).astype(BF16)
    half = total.shape[0] // 2
    return total[:half], total[half:]


def swap_edges(edge, plan):
    pairs = []
    for image in range(plan.batches):
        top = image * MOST_LAND // plan.share_rows
        bottom = (image * MOST_LAND + MOST_LAND - 1) // plan.share_rows
        for band in range(plan.bands - 1):
            upper = band * plan.sects + bottom
            lower = (band + 1) * plan.sects + top
            pairs += [(upper, lower), (lower, upper)]
    return lax.ppermute(edge, ("band", "sect"), pairs)


def swap_low_edges(low_level, band, bands):
    top, bottom = low_level[:, 0], low_level[:, -1]
    even = band % 2 == 0
    first_pairs = [(b, b ^ 1) for b in range(bands) if b ^ 1 < bands]
    second_pairs = []
    for b in range(1, bands - 1, 2):
        second_pairs += [(b, b + 1), (b + 1, b)]
    first = lax.ppermute(jnp.where(even, bottom, top), "band", first_pairs)
    second = lax.ppermute(jnp.where(even, top, bottom), "band", second_pairs)
    return first, second


def fits(batches, row_count, columns, bands, sects):
    slots = batches * MOST_LAND
    return (
        row_count == ROW_BLOCK
        and all(dilation % row_count == 0 for dilation in DILATIONS)
        and sects > 1
        and sects & (sects - 1) == 0
        and bands & (bands - 1) == 0
        and slots % sects == 0
        and MOST_LAND % (2 * (slots // sects)) == 0
        and columns % 16 == 0
        and batches <= 8
    )


def shards(
    features,
    low_level,
    land_mask,
    weight_one,
    weight_dilated,
    bias_branch,
    weight_pool,
    bias_pool,
    weight_project,
    bias_project,
    weight_reduce,
    bias_reduce,
    weight_merging,
    bias_merging,
):
    batches, row_count, columns, channels = features.shape
    bands, sects = lax.axis_size("band"), lax.axis_size("sect")
    plan = Plan(batches, row_count, columns, bands, sects)
    width = weight_one.shape[1]
    band, sect = lax.axis_index("band"), lax.axis_index("sect")
    place = jnp.stack([sect, band, jnp.int32(bands)]).astype(jnp.int32)
    far_masks = [
        lax.ppermute(land_mask, "band", [(target, source) for source, target in pairs])
        for _, _, _, pairs in plan.terms
    ]
    far_mask = jnp.stack(far_masks or [land_mask])
    pieces = branch_partials(
        plan, place, land_mask, far_mask, features, weight_one, weight_dilated
    )
    keep, send = pieces[:2]
    far_keep, far_send = pieces[2:] if plan.terms else (None, None)
    pool = call(
        pool_kernel,
        jax.ShapeDtypeStruct((8, width), F32),
        [VMEM, VMEM],
        [],
        3 * 16 * channels * width,
        2 * features.size,
    )(features, weight_pool)
    for bit in range(plan.bits):
        pattern = 1 << bit
        last = bit == plan.bits - 1
        if plan.terms:
            far_moved = swap(far_send, "sect", pattern)
            if last:
                far = (far_keep.astype(F32) + far_moved.astype(F32)).astype(BF16)
            else:
                far_keep, far_send = add_halves(far_keep, far_moved)
        moved = swap(send, "sect", pattern)
        if not last:
            keep, send = add_halves(keep, moved)
        pool = pool + swap(pool, "sect", pattern)
    far_terms = [
        lax.ppermute(far[:, term * width : (term + 1) * width], "band", pairs)
        for term, (_, _, _, pairs) in enumerate(plan.terms)
    ]
    for bit in reversed(range(bands.bit_length() - 1)):
        pool = pool + swap(pool, "band", 1 << bit)
    first, second = swap_low_edges(low_level, band, bands)
    reduced = weight_reduce.shape[1]
    low_part = call(
        low_kernel,
        jax.ShapeDtypeStruct((batches, row_count, columns, weight_merging.shape[3]), F32),
        [SMEM] + [VMEM] * 7,
        [pltpu.VMEM((batches, row_count + 2, columns, 3 * reduced), BF16)],
        2 * 3 * batches * row_count * columns * 256 * 256,
        4 * low_level.size,
    )(
        place,
        low_level,
        first,
        second,
        jnp.concatenate([weight_reduce] * 3, axis=1),
        jnp.concatenate([bias_reduce] * 3)[None],
        weight_merging[:, :, width:].reshape(3, 3 * reduced, -1),
        bias_merging[None],
    )
    share = jax.ShapeDtypeStruct((plan.share, width), BF16)
    row = jax.ShapeDtypeStruct((columns, width), BF16)
    out, edge = call(
        functools.partial(project_kernel, plan),
        (share, row),
        [SMEM, SMEM] + [VMEM] * (7 + len(plan.terms)),
        [pltpu.SMEM((batches * MOST_LAND,), jnp.int32), pltpu.VMEM((8, width), F32)],
        2 * plan.share * 4 * width * width,
        4 * plan.share * 4 * width + 2 * weight_project.size,
    )(
        place,
        land_mask,
        keep,
        moved,
        bias_branch,
        pool,
        bias_pool[None],
        weight_project,
        bias_project[None],
        *far_terms,
    )
    halo = swap_edges(edge, plan)
    shares = [out] + [swap(out, "sect", pattern) for pattern in range(1, sects)]
    halos = [halo] + [swap(halo, "sect", pattern) for pattern in range(1, sects)]
    live = batches * MOST_LAND * columns
    return call(
        functools.partial(merge_kernel, plan),
        jax.ShapeDtypeStruct(low_part.shape, BF16),
        [SMEM, SMEM] + [VMEM] * (2 + 2 * sects),
        [
            pltpu.SMEM((batches * MOST_LAND,), jnp.int32),
            pltpu.VMEM((live, 3 * width), BF16),
            pltpu.VMEM((sects * columns, 3 * width), BF16),
            pltpu.VMEM((batches, row_count + 2, columns, width), F32),
        ],
        2 * 9 * live * width * width,
        4 * low_part.size + 2 * weight_merging.size + 4 * live * width,
    )(place, land_mask, low_part, weight_merging, *shares, *halos)


def from_behind(value, axis, by):
    count = lax.axis_size(axis)
    pairs = [(i, i + by) for i in range(count) if 0 <= i + by < count]
    return lax.ppermute(value, axis, pairs)


def extended(block, sides, width):
    for axis, dim in sides:
        count = lax.axis_size(axis)
        forward = [(i, i + 1) for i in range(count - 1)]
        backward = [(target, source) for source, target in forward]
        low = lax.ppermute(
            lax.slice_in_dim(block, block.shape[dim] - width, None, axis=dim), axis, forward
        )
        high = lax.ppermute(lax.slice_in_dim(block, 0, width, axis=dim), axis, backward)
        block = jnp.concatenate([low, block, high], axis=dim)
    return block


def extend_rows(features):
    row_count = features.shape[1]
    reach_bands = min((PADDING + row_count - 1) // row_count, lax.axis_size("band") - 1)
    upper_blocks = []
    lower_blocks = []
    moving_up = features
    moving_down = features
    for hop_index in range(reach_bands):
        moving_up = from_behind(moving_up, "band", 1)
        moving_down = from_behind(moving_down, "band", -1)
        upper_blocks.insert(0, moving_up)
        lower_blocks.append(moving_down)
    margin = reach_bands * row_count
    stacked = jnp.concatenate(upper_blocks + [features] + lower_blocks, axis=1)
    if margin >= PADDING:
        stacked = stacked[:, margin - PADDING : margin + row_count + PADDING]
    else:
        stacked = jnp.pad(stacked, ((0, 0), (PADDING - margin, PADDING - margin), (0, 0), (0, 0)))
    return jnp.pad(stacked, ((0, 0), (0, 0), (PADDING, PADDING), (0, 0)))


def branch_terms(window, select_rows, weight_one, weight_dilated, live_rows, col_count):
    batches = window.shape[0]
    channels = window.shape[3]
    centre = select_rows(0)[:, :, PADDING : PADDING + col_count].reshape(-1, channels)
    partials = [jnp.dot(centre, weight_one, preferred_element_type=jnp.float32)]
    for branch_index, dilation in enumerate(DILATIONS):
        running = jnp.zeros((centre.shape[0], weight_one.shape[1]), jnp.float32)
        for row_tap in range(3):
            band_rows = select_rows(dilation * (row_tap - 1))
            for col_tap in range(3):
                left = PADDING + dilation * (col_tap - 1)
                tap_rows = band_rows[:, :, left : left + col_count].reshape(-1, channels)
                running = running + jnp.dot(
                    tap_rows,
                    weight_dilated[branch_index, row_tap, col_tap],
                    preferred_element_type=jnp.float32,
                )
        partials.append(running)
    return jnp.concatenate(partials, axis=1).reshape(batches, live_rows, col_count, -1)


def pool_context(features, weight_pool, bias_pool, row_count, col_count):
    local_sum = jnp.sum(features, axis=(1, 2), dtype=jnp.float32)
    cell_count = row_count * lax.axis_size("band") * col_count
    weight_full = weight_pool.astype(jnp.float32)
    average = lax.psum(local_sum, "band") / cell_count
    pre_relu = lax.psum(jnp.dot(average, weight_full, precision=PRECISE), "sect")
    return jax.nn.relu(pre_relu + bias_pool)


def general_shards(
    features,
    low_level,
    land_mask,
    weight_one,
    weight_dilated,
    bias_branch,
    weight_pool,
    bias_pool,
    weight_project,
    bias_project,
    weight_reduce,
    bias_reduce,
    weight_merging,
    bias_merging,
):
    batches, row_count, col_count, channels = features.shape
    branch_width = weight_project.shape[1]
    window = extend_rows(features)
    pooled = pool_context(features, weight_pool, bias_pool, row_count, col_count)
    context = jnp.dot(
        pooled, weight_project[4 * branch_width :].astype(jnp.float32), precision=PRECISE
    )
    row_mask = land_mask.astype(jnp.float32)

    def select_rows(offset):
        return window[:, PADDING + offset : PADDING + offset + row_count]

    partials = branch_terms(window, select_rows, weight_one, weight_dilated, row_count, col_count)
    flat_terms = partials.astype(jnp.bfloat16).reshape(-1, partials.shape[3])
    summed_cells = lax.psum_scatter(flat_terms, "sect", scatter_dimension=0, tiled=True).astype(
        jnp.float32
    )
    share_cells = summed_cells.shape[0]
    first_cell = lax.axis_index("sect") * share_cells
    branch_cells = jax.nn.relu(summed_cells + bias_branch.reshape(-1)).astype(jnp.bfloat16)
    projected_cells = jnp.dot(
        branch_cells, weight_project[: 4 * branch_width], preferred_element_type=jnp.float32
    )
    cell_ids = first_cell + lax.broadcasted_iota(jnp.int32, (share_cells,), 0)
    batch_of = cell_ids // (row_count * col_count)
    batch_onehot = (batch_of[:, None] == lax.broadcasted_iota(jnp.int32, (1, batches), 1)).astype(
        jnp.float32
    )
    context_cells = jnp.dot(batch_onehot, context, precision=PRECISE)
    keep_all = jnp.broadcast_to(row_mask[:, :, None], (batches, row_count, col_count)).reshape(-1)
    keep_cells = lax.dynamic_slice_in_dim(keep_all, first_cell, share_cells, 0)
    out_cells = (
        jax.nn.relu(projected_cells + context_cells + bias_project) * keep_cells[:, None]
    ).astype(jnp.bfloat16)
    project_out = lax.all_gather(out_cells, "sect", axis=0, tiled=True).reshape(
        batches, row_count, col_count, branch_width
    )
    low_reduced = (
        jax.nn.relu(
            jnp.dot(
                low_level.reshape(-1, low_level.shape[3]),
                weight_reduce,
                preferred_element_type=jnp.float32,
            )
            + bias_reduce
        )
        .astype(jnp.bfloat16)
        .reshape(batches, row_count, col_count, -1)
    )
    joined = jnp.concatenate([project_out, low_reduced], axis=3)
    framed = extended(joined, (("band", 1),), 1)
    framed = jnp.pad(framed, ((0, 0), (0, 0), (1, 1), (0, 0)))
    running = jnp.zeros((batches * row_count * col_count, weight_merging.shape[3]), jnp.float32)
    for row_tap in range(3):
        for col_tap in range(3):
            tap_rows = framed[
                :, row_tap : row_tap + row_count, col_tap : col_tap + col_count
            ].reshape(-1, joined.shape[3])
            running = running + jnp.dot(
                tap_rows, weight_merging[row_tap, col_tap], preferred_element_type=jnp.float32
            )
    merged_map = (
        jax.nn.relu(running + bias_merging).reshape(batches, row_count, col_count, -1)
        * row_mask[:, :, None, None]
    )
    return merged_map.astype(jnp.bfloat16)


def solution(mesh):
    in_specs = (
        P("grp", "band", None, "sect"),
        P("grp", "band", None, None),
        P("grp", "band"),
        P("sect", None),
        P(None, None, None, "sect", None),
        P(),
        P("sect", None),
        P(),
        P(),
        P(),
        P(),
        P(),
        P(),
        P(),
    )
    out_specs = P("grp", "band", None, None)

    def chosen(features, *others):
        batches, row_count, columns, _ = features.shape
        sizes = (batches, row_count, columns, mesh.shape["band"], mesh.shape["sect"])
        body = shards if fits(*sizes) else general_shards
        return body(features, *others)

    return jax.shard_map(
        chosen, mesh=mesh, in_specs=in_specs, out_specs=out_specs, check_vma=False
    )
```

```python
import functools

import jax
import jax.numpy as jnp
from jax import lax
from jax.experimental import pallas as pl
from jax.experimental.pallas import tpu as pltpu
from jax.sharding import PartitionSpec as P

DILATIONS = (12, 24, 36)
PADDING = 36
PRECISE = lax.Precision.HIGHEST
ROW_BLOCK = 6
MOST_LAND = 4
VMEM_LIMIT = 32 * 2 ** 20
WHOLE_VMEM = 60 * 2 ** 20
EARLY = 2
F32 = jnp.float32
BF16 = jnp.bfloat16
VMEM = pl.BlockSpec(memory_space=pltpu.VMEM)
HBM = pl.BlockSpec(memory_space=pltpu.HBM)


def call(body, outs, in_specs, scratch, flops, bytes_accessed, limit=VMEM_LIMIT):
    return pl.pallas_call(
        body,
        out_shape=outs,
        in_specs=in_specs,
        out_specs=jax.tree.map(lambda _: VMEM, outs),
        scratch_shapes=scratch,
        compiler_params=pltpu.CompilerParams(vmem_limit_bytes=limit),
        cost_estimate=pl.CostEstimate(
            flops=flops, bytes_accessed=bytes_accessed, transcendentals=0
        ),
    )


def reversed_bits(value, bits):
    return sum(((value >> bit) & 1) << (bits - 1 - bit) for bit in range(bits))


def fill_slots(mask_ref, slots_ref, batches, row_count):
    for image in range(batches):
        inner = range(1, row_count - 1)
        lives = {row: (mask_ref[image, row] > 0).astype(jnp.int32) for row in inner}
        land_total = sum(lives.values())
        land_before, sea_before = 0, 0
        chosen = [0] * (MOST_LAND - 2)
        for row in inner:
            live = lives[row]
            rank = jnp.where(live > 0, land_before, land_total + sea_before)
            chosen = [
                value + row * (rank == slot).astype(jnp.int32)
                for slot, value in enumerate(chosen)
            ]
            land_before = land_before + live
            sea_before = sea_before + (1 - live)
        base = image * MOST_LAND
        rows = [jnp.int32(0), *chosen, jnp.int32(row_count - 1)]
        flags = [(land_total > slot).astype(jnp.int32) for slot in range(MOST_LAND - 2)]
        flags = [mask_ref[image, 0], *flags, mask_ref[image, row_count - 1]]
        for slot in range(MOST_LAND):
            slots_ref[0, base + slot] = rows[slot]
            slots_ref[1, base + slot] = flags[slot]


def split_three(value):
    high = value.astype(BF16)
    rest = value - high.astype(F32)
    middle = rest.astype(BF16)
    low = (rest - middle.astype(F32)).astype(BF16)
    return high, middle, low


def precise_dot(value, weight):
    return sum(jnp.dot(part, weight, preferred_element_type=F32) for part in split_three(value))


def shifted(value, by, columns):
    blocks = value.reshape(-1, columns, value.shape[1])
    empty = jnp.zeros((blocks.shape[0], abs(by), value.shape[1]), value.dtype)
    if by > 0:
        moved = jnp.concatenate([empty, blocks[:, : columns - by]], axis=1)
    else:
        moved = jnp.concatenate([blocks[:, -by:], empty], axis=1)
    return moved.reshape(value.shape)


class Plan:
    def __init__(self, batches, row_count, columns, bands, sects):
        self.batches, self.row_count, self.columns = batches, row_count, columns
        self.bands, self.sects = bands, sects
        self.bits = sects.bit_length() - 1
        self.share_rows = batches * MOST_LAND // sects
        self.share = self.share_rows * columns
        self.terms = []
        for branch, dilation in enumerate(DILATIONS):
            hop = dilation // row_count
            if hop >= bands:
                continue
            up = [(b, b + hop) for b in range(bands - hop)]
            down = [(target, source) for source, target in up]
            if 2 * hop >= bands:
                self.terms.append((branch, hop, None, up + down))
            else:
                self.terms.append((branch, hop, 0, up))
                self.terms.append((branch, hop, 2, down))

    def rows_of(self, position, sect, slots_ref):
        owner = sect ^ reversed_bits(position, self.bits)
        for row in range(self.share_rows):
            place = owner * self.share_rows + row
            start = (position * self.share_rows + row) * self.columns
            yield lax.div(place, MOST_LAND), slots_ref[0, place], start


def tap_sum(rows, taps, dilation, columns):
    width = taps.shape[1] // 3
    if dilation >= columns:
        return jnp.dot(rows, taps[:, width : 2 * width], preferred_element_type=F32)
    result = jnp.dot(rows, taps, preferred_element_type=F32)
    return (
        result[:, width : 2 * width]
        + shifted(result[:, :width], dilation, columns)
        + shifted(result[:, 2 * width :], -dilation, columns)
    )


def store_halves(keep, send, index, value):
    half, width = keep.shape[0], value.shape[1]
    value = value.astype(BF16)
    keep[:, pl.ds(index * width, width)] = value[:half]
    send[:, pl.ds(index * width, width)] = value[half:]


def early_kernel(plan, mask_ref, features_ref, dilated_ref, keep, send, slots_ref, land_ref, rows_ref, taps_ref, mask_sem, row_sems, tap_sems):
    columns, width = plan.columns, dilated_ref.shape[4]
    mask_copy = pltpu.make_async_copy(mask_ref, land_ref, mask_sem)
    mask_copy.start()
    branches = range(EARLY - 1, len(DILATIONS))
    tap_copies = []
    for index, branch in enumerate(branches):
        tap_copies.append([])
        for tap in range(3):
            copy = pltpu.make_async_copy(
                dilated_ref.at[branch, 1, tap],
                taps_ref.at[index, :, pl.ds(tap * width, width)],
                tap_sems.at[index, tap],
            )
            copy.start()
            tap_copies[-1].append(copy)
    mask_copy.wait()
    fill_slots(land_ref, slots_ref, plan.batches, plan.row_count)
    row_copies = []
    sect = lax.axis_index("sect")
    for position in range(plan.sects):
        for image, row, start in plan.rows_of(position, sect, slots_ref):
            copy = pltpu.make_async_copy(
                features_ref.at[image, row],
                rows_ref.at[pl.ds(start, columns)],
                row_sems.at[start // columns],
            )
            copy.start()
            row_copies.append(copy)
    for copy in row_copies:
        copy.wait()
    for index, branch in enumerate(branches):
        for copy in tap_copies[index]:
            copy.wait()
        value = tap_sum(rows_ref[...], taps_ref[index], DILATIONS[branch], columns)
        store_halves(keep, send, index, value)


def early_partials(plan, mask, features, weight_dilated):
    channels, width = weight_dilated.shape[3:]
    half = plan.sects // 2 * plan.share
    branches = len(DILATIONS) + 1 - EARLY
    out = jax.ShapeDtypeStruct((half, branches * width), BF16)
    slots = plan.batches * MOST_LAND
    scratch = [
        pltpu.SMEM((2, slots), jnp.int32),
        pltpu.SMEM(mask.shape, jnp.int32),
        pltpu.VMEM((2 * half, channels), BF16),
        pltpu.VMEM((branches, channels, 3 * width), BF16),
        pltpu.SemaphoreType.DMA,
        pltpu.SemaphoreType.DMA((slots,)),
        pltpu.SemaphoreType.DMA((branches, 3)),
    ]
    return call(
        functools.partial(early_kernel, plan),
        (out, out),
        [HBM, HBM, HBM],
        scratch,
        2 * 3 * branches * 2 * half * channels * width,
        2 * (3 * branches * channels * width + 2 * half * channels),
        WHOLE_VMEM,
    )(mask, features, weight_dilated)


def late_kernel(plan, needed, mask_ref, far_mask_ref, features_ref, one_ref, *refs):
    terms = len(plan.terms)
    dilated = dict(zip(needed, refs[: len(needed)]))
    refs = refs[len(needed) :]
    outs = refs[: 2 + (2 if terms else 0)]
    slots_ref, rows_ref = refs[len(outs) :]
    sect, band = lax.axis_index("sect"), lax.axis_index("band")

    def gather(mask):
        fill_slots(mask, slots_ref, plan.batches, plan.row_count)
        for position in range(plan.sects):
            for image, row, start in plan.rows_of(position, sect, slots_ref):
                rows_ref[pl.ds(start, plan.columns)] = features_ref[image, row]

    def taps_of(branch, row_tap):
        return jnp.concatenate([dilated[branch][row_tap, tap] for tap in range(3)], axis=1)

    for term, (branch, hop, row_tap, _) in enumerate(plan.terms):
        gather(far_mask_ref.at[term])
        if row_tap is None:
            row_tap = jnp.where(band + hop < plan.bands, 0, 2)
        taps = taps_of(branch, row_tap)
        value = tap_sum(rows_ref[...], taps, DILATIONS[branch], plan.columns)
        store_halves(outs[2], outs[3], term, value)
    gather(mask_ref)
    value = jnp.dot(rows_ref[...], one_ref[...], preferred_element_type=F32)
    store_halves(outs[0], outs[1], 0, value)
    for branch in range(EARLY - 1):
        value = tap_sum(rows_ref[...], taps_of(branch, 1), DILATIONS[branch], plan.columns)
        store_halves(outs[0], outs[1], branch + 1, value)


def late_partials(plan, mask, far_mask, features, weight_one, weight_dilated):
    terms = len(plan.terms)
    channels, width = weight_one.shape
    half = plan.sects // 2 * plan.share
    own = jax.ShapeDtypeStruct((half, EARLY * width), BF16)
    outs = [own, own]
    if terms:
        far = jax.ShapeDtypeStruct((half, terms * width), BF16)
        outs += [far, far]
    needed = sorted({term[0] for term in plan.terms} | set(range(EARLY - 1)))
    products = 1 + 3 * (EARLY - 1 + terms)
    return call(
        functools.partial(late_kernel, plan, needed),
        tuple(outs),
        [VMEM] * (4 + len(needed)),
        [
            pltpu.SMEM((2, plan.batches * MOST_LAND), jnp.int32),
            pltpu.VMEM((2 * half, channels), BF16),
        ],
        2 * products * 2 * half * channels * width,
        2 * (9 * len(needed) * channels * width + features.size),
    )(mask, far_mask, features, weight_one, *[weight_dilated[branch] for branch in needed])


def pool_kernel(features_ref, weight_ref, out_ref):
    batches, row_count, columns, channels = features_ref.shape
    sums = [
        jnp.sum(
            features_ref[image].astype(F32).reshape(row_count * columns, channels),
            axis=0,
            keepdims=True,
        )
        for image in range(batches)
    ]
    row = lax.broadcasted_iota(jnp.int32, (out_ref.shape[0], channels), 0)
    stacked = jnp.zeros((out_ref.shape[0], channels), F32)
    for image, value in enumerate(sums):
        stacked = jnp.where(row == image, value, stacked)
    out_ref[...] = precise_dot(stacked, weight_ref[...])


def low_kernel(plan, low_ref, first_ref, second_ref, reduce_ref, bias_reduce_ref, merging_ref, bias_ref, out_ref, framed_ref):
    batches, row_count, columns, depth = low_ref.shape
    band, bands = lax.axis_index("band"), plan.bands
    wide = reduce_ref.shape[1]
    reduced = wide // 3
    even = lax.rem(band, 2) == 0

    def reduce(rows):
        value = jnp.dot(rows, reduce_ref[...], preferred_element_type=F32) + bias_reduce_ref[...]
        value = jnp.maximum(value, 0.0).astype(BF16).astype(F32)
        lane = lax.broadcasted_iota(jnp.int32, value.shape, 1)
        return jnp.where(
            lane < reduced,
            shifted(value, 1, columns),
            jnp.where(lane < 2 * reduced, value, shifted(value, -1, columns)),
        )

    framed_ref[:, 1 : row_count + 1] = (
        reduce(low_ref[...].reshape(-1, depth)).astype(BF16).reshape(batches, row_count, columns, wide)
    )
    first = reduce(first_ref[...].reshape(-1, depth))
    second = reduce(second_ref[...].reshape(-1, depth))
    above = jnp.where(even, second, first) * jnp.where(band > 0, 1.0, 0.0)
    below = jnp.where(even, first, second) * jnp.where(band < bands - 1, 1.0, 0.0)
    framed_ref[:, 0] = above.astype(BF16).reshape(batches, columns, wide)
    framed_ref[:, row_count + 1] = below.astype(BF16).reshape(batches, columns, wide)
    for image in range(batches):
        total = jnp.zeros((row_count * columns, out_ref.shape[3]), F32) + bias_ref[...]
        for tap in range(3):
            rows = framed_ref[image, tap : tap + row_count].reshape(-1, wide)
            total = total + jnp.dot(rows, merging_ref[tap], preferred_element_type=F32)
        out_ref[image] = total.reshape(row_count, columns, -1)


def project_kernel(plan, mask_ref, keep_ref, moved_ref, early_keep_ref, early_moved_ref, bias_branch_ref, pool_ref, bias_pool_ref, weight_ref, bias_ref, *refs):
    far_refs = refs[: len(plan.terms)]
    out_ref, edge_ref, slots_ref, context_ref = refs[len(plan.terms) :]
    columns, width = plan.columns, weight_ref.shape[1]
    sect = lax.axis_index("sect")
    fill_slots(mask_ref, slots_ref, plan.batches, plan.row_count)
    cells = plan.row_count * plan.bands * columns
    pooled = jnp.maximum(pool_ref[...] / cells + bias_pool_ref[...], 0.0)
    context_ref[...] = precise_dot(pooled, weight_ref[4 * width :]) + bias_ref[...]
    total = jnp.zeros((plan.share, width), F32)
    for branch in range(4):
        early = branch >= EARLY
        kept, added = (early_keep_ref, early_moved_ref) if early else (keep_ref, moved_ref)
        lanes = pl.ds((branch - EARLY if early else branch) * width, width)
        value = kept[:, lanes].astype(F32) + added[:, lanes].astype(F32)
        for term, far in zip(plan.terms, far_refs):
            if term[0] + 1 == branch:
                value = value + far[...].astype(F32)
        value = jnp.maximum(value + bias_branch_ref[pl.ds(branch, 1)], 0.0).astype(BF16)
        total = total + jnp.dot(
            value, weight_ref[pl.ds(branch * width, width)], preferred_element_type=F32
        )
    for row in range(plan.share_rows):
        place = sect * plan.share_rows + row
        image = lax.div(place, MOST_LAND)
        keep = slots_ref[1, place].astype(F32)
        value = total[row * columns : (row + 1) * columns] + context_ref[pl.ds(image, 1)]
        out_ref[pl.ds(row * columns, columns)] = (jnp.maximum(value, 0.0) * keep).astype(BF16)
    at_top = lax.rem(sect * plan.share_rows, MOST_LAND) == 0

    @pl.when(at_top)
    def _():
        edge_ref[...] = out_ref[pl.ds(0, columns)]

    @pl.when(jnp.logical_not(at_top))
    def _():
        edge_ref[...] = out_ref[pl.ds(plan.share - columns, columns)]


def merge_kernel(plan, mask_ref, low_ref, weight_ref, *refs):
    sects, columns = plan.sects, plan.columns
    share_refs, edge_refs = refs[:sects], refs[sects : 2 * sects]
    out_ref, slots_ref, rows_ref, halo_ref, total_ref = refs[2 * sects :]
    width = weight_ref.shape[3]
    sect = lax.axis_index("sect")
    fill_slots(mask_ref, slots_ref, plan.batches, plan.row_count)

    def spread(value):
        wide = value.astype(F32)
        return (
            shifted(wide, 1, columns).astype(BF16),
            value,
            shifted(wide, -1, columns).astype(BF16),
        )

    def weight(tap):
        return jnp.concatenate([weight_ref[tap, side, :width] for side in range(3)], axis=0)

    total_ref[:, 1 : plan.row_count + 1] = low_ref[...]
    tops, bottoms = [], []
    for offset in range(sects):
        for side, value in enumerate(spread(share_refs[offset][...])):
            rows_ref[pl.ds(offset * plan.share, plan.share), pl.ds(side * width, width)] = value
        for side, value in enumerate(spread(edge_refs[offset][...])):
            halo_ref[pl.ds(offset * columns, columns), pl.ds(side * width, width)] = value
    for tap in range(3):
        taps = weight(tap)
        result = jnp.dot(rows_ref[...], taps, preferred_element_type=F32)
        if tap != 1:
            halo = jnp.dot(halo_ref[...], taps, preferred_element_type=F32)
        for offset in range(sects):
            owner = sect ^ offset
            for row in range(plan.share_rows):
                place = owner * plan.share_rows + row
                image = lax.div(place, MOST_LAND)
                at = slots_ref[0, place] + 2 - tap
                start = (offset * plan.share_rows + row) * columns
                total_ref[image, at] = total_ref[image, at] + result[start : start + columns]
            first = owner * plan.share_rows
            image = lax.div(first, MOST_LAND)
            top = lax.rem(first, MOST_LAND) == 0
            bottom = lax.rem(first + plan.share_rows, MOST_LAND) == 0
            if tap != 1:
                piece = halo[offset * columns : (offset + 1) * columns]
                at = 1 if tap == 0 else plan.row_count
                factor = jnp.where(top if tap == 0 else bottom, 1.0, 0.0)
                total_ref[image, at] = total_ref[image, at] + piece * factor
    for image in range(plan.batches):
        for row in range(plan.row_count):
            keep = mask_ref[image, row].astype(F32)
            out_ref[image, row] = (jnp.maximum(total_ref[image, row + 1], 0.0) * keep).astype(BF16)


def swap(value, axis, pattern):
    count = lax.axis_size(axis)
    return lax.ppermute(value, axis, [(i, i ^ pattern) for i in range(count)])


def add_halves(keep, moved):
    total = (keep.astype(F32) + moved.astype(F32)).astype(BF16)
    half = total.shape[0] // 2
    return total[:half], total[half:]


def swap_edges(edge, plan):
    pairs = []
    for image in range(plan.batches):
        top = image * MOST_LAND // plan.share_rows
        bottom = (image * MOST_LAND + MOST_LAND - 1) // plan.share_rows
        for band in range(plan.bands - 1):
            upper = band * plan.sects + bottom
            lower = (band + 1) * plan.sects + top
            pairs += [(upper, lower), (lower, upper)]
    return lax.ppermute(edge, ("band", "sect"), pairs)


def swap_low_edges(low_level, band, bands):
    top, bottom = low_level[:, 0], low_level[:, -1]
    even = band % 2 == 0
    first_pairs = [(b, b ^ 1) for b in range(bands) if b ^ 1 < bands]
    second_pairs = []
    for b in range(1, bands - 1, 2):
        second_pairs += [(b, b + 1), (b + 1, b)]
    first = lax.ppermute(jnp.where(even, bottom, top), "band", first_pairs)
    second = lax.ppermute(jnp.where(even, top, bottom), "band", second_pairs)
    return first, second


def fits(batches, row_count, columns, bands, sects):
    slots = batches * MOST_LAND
    return (
        row_count == ROW_BLOCK
        and all(dilation % row_count == 0 for dilation in DILATIONS)
        and sects > 1
        and sects & (sects - 1) == 0
        and bands & (bands - 1) == 0
        and slots % sects == 0
        and MOST_LAND % (2 * (slots // sects)) == 0
        and columns % 16 == 0
        and batches <= 8
    )


def shards(
    features,
    low_level,
    land_mask,
    weight_one,
    weight_dilated,
    bias_branch,
    weight_pool,
    bias_pool,
    weight_project,
    bias_project,
    weight_reduce,
    bias_reduce,
    weight_merging,
    bias_merging,
):
    batches, row_count, columns, channels = features.shape
    bands, sects = lax.axis_size("band"), lax.axis_size("sect")
    plan = Plan(batches, row_count, columns, bands, sects)
    width = weight_one.shape[1]
    band = lax.axis_index("band")
    early_keep, early_send = early_partials(plan, land_mask, features, weight_dilated)
    early_keep, early_send, later_mask, later_features, later_low = lax.optimization_barrier(
        (early_keep, early_send, land_mask, features, low_level)
    )
    pool = call(
        pool_kernel,
        jax.ShapeDtypeStruct((8, width), F32),
        [VMEM, VMEM],
        [],
        3 * 16 * channels * width,
        2 * features.size,
    )(later_features, weight_pool)
    early_moved = swap(early_send, "sect", 1)
    far_masks = [
        lax.ppermute(later_mask, "band", [(target, source) for source, target in pairs])
        for _, _, _, pairs in plan.terms
    ]
    pool_bits = list(range(bands.bit_length() - 1))
    if pool_bits:
        pool = pool + swap(pool, "band", 1 << pool_bits.pop())
    far_mask = jnp.stack(far_masks or [land_mask])
    for bit in range(1, plan.bits):
        early_keep, early_send = add_halves(early_keep, early_moved)
        early_moved = swap(early_send, "sect", 1 << bit)
    for bit in range(1, plan.bits):
        pool = pool + swap(pool, "sect", 1 << bit)
    pieces = late_partials(
        plan, later_mask, far_mask, later_features, weight_one, weight_dilated
    )
    keep, send = pieces[:2]
    far_keep, far_send = pieces[2:] if plan.terms else (None, None)
    pool = pool + swap(pool, "sect", 1)
    for bit in range(plan.bits):
        pattern = 1 << bit
        last = bit == plan.bits - 1
        if plan.terms:
            far_moved = swap(far_send, "sect", pattern)
            if last:
                far = (far_keep.astype(F32) + far_moved.astype(F32)).astype(BF16)
            else:
                far_keep, far_send = add_halves(far_keep, far_moved)
        moved = swap(send, "sect", pattern)
        if not last:
            keep, send = add_halves(keep, moved)
    far_terms = [
        lax.ppermute(far[:, term * width : (term + 1) * width], "band", pairs)
        for term, (_, _, _, pairs) in enumerate(plan.terms)
    ]
    first, second = swap_low_edges(later_low, band, bands)
    for bit in reversed(pool_bits):
        pool = pool + swap(pool, "band", 1 << bit)
    reduced = weight_reduce.shape[1]
    low_part = call(
        functools.partial(low_kernel, plan),
        jax.ShapeDtypeStruct((batches, row_count, columns, weight_merging.shape[3]), F32),
        [VMEM] * 7,
        [pltpu.VMEM((batches, row_count + 2, columns, 3 * reduced), BF16)],
        2 * 3 * batches * row_count * columns * 256 * 256,
        4 * low_level.size,
    )(
        later_low,
        first,
        second,
        jnp.concatenate([weight_reduce] * 3, axis=1),
        jnp.concatenate([bias_reduce] * 3)[None],
        weight_merging[:, :, width:].reshape(3, 3 * reduced, -1),
        bias_merging[None],
    )
    share = jax.ShapeDtypeStruct((plan.share, width), BF16)
    row = jax.ShapeDtypeStruct((columns, width), BF16)
    out, edge = call(
        functools.partial(project_kernel, plan),
        (share, row),
        [VMEM] * (10 + len(plan.terms)),
        [pltpu.SMEM((2, batches * MOST_LAND), jnp.int32), pltpu.VMEM((8, width), F32)],
        2 * plan.share * 4 * width * width,
        4 * plan.share * 4 * width + 2 * weight_project.size,
    )(
        land_mask,
        keep,
        moved,
        early_keep,
        early_moved,
        bias_branch,
        pool,
        bias_pool[None],
        weight_project,
        bias_project[None],
        *far_terms,
    )
    halo = swap_edges(edge, plan)
    shares = [out] + [swap(out, "sect", pattern) for pattern in range(1, sects)]
    halos = [halo] + [swap(halo, "sect", pattern) for pattern in range(1, sects)]
    live = batches * MOST_LAND * columns
    return call(
        functools.partial(merge_kernel, plan),
        jax.ShapeDtypeStruct(low_part.shape, BF16),
        [VMEM] * (3 + 2 * sects),
        [
            pltpu.SMEM((2, batches * MOST_LAND), jnp.int32),
            pltpu.VMEM((live, 3 * width), BF16),
            pltpu.VMEM((sects * columns, 3 * width), BF16),
            pltpu.VMEM((batches, row_count + 2, columns, width), F32),
        ],
        2 * 9 * live * width * width,
        4 * low_part.size + 2 * weight_merging.size + 4 * live * width,
    )(land_mask, low_part, weight_merging, *shares, *halos)


def from_behind(value, axis, by):
    count = lax.axis_size(axis)
    pairs = [(i, i + by) for i in range(count) if 0 <= i + by < count]
    return lax.ppermute(value, axis, pairs)


def extended(block, sides, width):
    for axis, dim in sides:
        count = lax.axis_size(axis)
        forward = [(i, i + 1) for i in range(count - 1)]
        backward = [(target, source) for source, target in forward]
        low = lax.ppermute(
            lax.slice_in_dim(block, block.shape[dim] - width, None, axis=dim), axis, forward
        )
        high = lax.ppermute(lax.slice_in_dim(block, 0, width, axis=dim), axis, backward)
        block = jnp.concatenate([low, block, high], axis=dim)
    return block


def extend_rows(features):
    row_count = features.shape[1]
    reach_bands = min((PADDING + row_count - 1) // row_count, lax.axis_size("band") - 1)
    upper_blocks = []
    lower_blocks = []
    moving_up = features
    moving_down = features
    for hop_index in range(reach_bands):
        moving_up = from_behind(moving_up, "band", 1)
        moving_down = from_behind(moving_down, "band", -1)
        upper_blocks.insert(0, moving_up)
        lower_blocks.append(moving_down)
    margin = reach_bands * row_count
    stacked = jnp.concatenate(upper_blocks + [features] + lower_blocks, axis=1)
    if margin >= PADDING:
        stacked = stacked[:, margin - PADDING : margin + row_count + PADDING]
    else:
        stacked = jnp.pad(stacked, ((0, 0), (PADDING - margin, PADDING - margin), (0, 0), (0, 0)))
    return jnp.pad(stacked, ((0, 0), (0, 0), (PADDING, PADDING), (0, 0)))


def branch_terms(window, select_rows, weight_one, weight_dilated, live_rows, col_count):
    batches = window.shape[0]
    channels = window.shape[3]
    centre = select_rows(0)[:, :, PADDING : PADDING + col_count].reshape(-1, channels)
    partials = [jnp.dot(centre, weight_one, preferred_element_type=jnp.float32)]
    for branch_index, dilation in enumerate(DILATIONS):
        running = jnp.zeros((centre.shape[0], weight_one.shape[1]), jnp.float32)
        for row_tap in range(3):
            band_rows = select_rows(dilation * (row_tap - 1))
            for col_tap in range(3):
                left = PADDING + dilation * (col_tap - 1)
                tap_rows = band_rows[:, :, left : left + col_count].reshape(-1, channels)
                running = running + jnp.dot(
                    tap_rows,
                    weight_dilated[branch_index, row_tap, col_tap],
                    preferred_element_type=jnp.float32,
                )
        partials.append(running)
    return jnp.concatenate(partials, axis=1).reshape(batches, live_rows, col_count, -1)


def pool_context(features, weight_pool, bias_pool, row_count, col_count):
    local_sum = jnp.sum(features, axis=(1, 2), dtype=jnp.float32)
    cell_count = row_count * lax.axis_size("band") * col_count
    weight_full = weight_pool.astype(jnp.float32)
    average = lax.psum(local_sum, "band") / cell_count
    pre_relu = lax.psum(jnp.dot(average, weight_full, precision=PRECISE), "sect")
    return jax.nn.relu(pre_relu + bias_pool)


def general_shards(
    features,
    low_level,
    land_mask,
    weight_one,
    weight_dilated,
    bias_branch,
    weight_pool,
    bias_pool,
    weight_project,
    bias_project,
    weight_reduce,
    bias_reduce,
    weight_merging,
    bias_merging,
):
    batches, row_count, col_count, channels = features.shape
    branch_width = weight_project.shape[1]
    window = extend_rows(features)
    pooled = pool_context(features, weight_pool, bias_pool, row_count, col_count)
    context = jnp.dot(
        pooled, weight_project[4 * branch_width :].astype(jnp.float32), precision=PRECISE
    )
    row_mask = land_mask.astype(jnp.float32)

    def select_rows(offset):
        return window[:, PADDING + offset : PADDING + offset + row_count]

    partials = branch_terms(window, select_rows, weight_one, weight_dilated, row_count, col_count)
    flat_terms = partials.astype(jnp.bfloat16).reshape(-1, partials.shape[3])
    summed_cells = lax.psum_scatter(flat_terms, "sect", scatter_dimension=0, tiled=True).astype(
        jnp.float32
    )
    share_cells = summed_cells.shape[0]
    first_cell = lax.axis_index("sect") * share_cells
    branch_cells = jax.nn.relu(summed_cells + bias_branch.reshape(-1)).astype(jnp.bfloat16)
    projected_cells = jnp.dot(
        branch_cells, weight_project[: 4 * branch_width], preferred_element_type=jnp.float32
    )
    cell_ids = first_cell + lax.broadcasted_iota(jnp.int32, (share_cells,), 0)
    batch_of = cell_ids // (row_count * col_count)
    batch_onehot = (batch_of[:, None] == lax.broadcasted_iota(jnp.int32, (1, batches), 1)).astype(
        jnp.float32
    )
    context_cells = jnp.dot(batch_onehot, context, precision=PRECISE)
    keep_all = jnp.broadcast_to(row_mask[:, :, None], (batches, row_count, col_count)).reshape(-1)
    keep_cells = lax.dynamic_slice_in_dim(keep_all, first_cell, share_cells, 0)
    out_cells = (
        jax.nn.relu(projected_cells + context_cells + bias_project) * keep_cells[:, None]
    ).astype(jnp.bfloat16)
    project_out = lax.all_gather(out_cells, "sect", axis=0, tiled=True).reshape(
        batches, row_count, col_count, branch_width
    )
    low_reduced = (
        jax.nn.relu(
            jnp.dot(
                low_level.reshape(-1, low_level.shape[3]),
                weight_reduce,
                preferred_element_type=jnp.float32,
            )
            + bias_reduce
        )
        .astype(jnp.bfloat16)
        .reshape(batches, row_count, col_count, -1)
    )
    joined = jnp.concatenate([project_out, low_reduced], axis=3)
    framed = extended(joined, (("band", 1),), 1)
    framed = jnp.pad(framed, ((0, 0), (0, 0), (1, 1), (0, 0)))
    running = jnp.zeros((batches * row_count * col_count, weight_merging.shape[3]), jnp.float32)
    for row_tap in range(3):
        for col_tap in range(3):
            tap_rows = framed[
                :, row_tap : row_tap + row_count, col_tap : col_tap + col_count
            ].reshape(-1, joined.shape[3])
            running = running + jnp.dot(
                tap_rows, weight_merging[row_tap, col_tap], preferred_element_type=jnp.float32
            )
    merged_map = (
        jax.nn.relu(running + bias_merging).reshape(batches, row_count, col_count, -1)
        * row_mask[:, :, None, None]
    )
    return merged_map.astype(jnp.bfloat16)


def solution(mesh):
    in_specs = (
        P("grp", "band", None, "sect"),
        P("grp", "band", None, None),
        P("grp", "band"),
        P("sect", None),
        P(None, None, None, "sect", None),
        P(),
        P("sect", None),
        P(),
        P(),
        P(),
        P(),
        P(),
        P(),
        P(),
    )
    out_specs = P("grp", "band", None, None)

    def chosen(features, *others):
        batches, row_count, columns, _ = features.shape
        sizes = (batches, row_count, columns, mesh.shape["band"], mesh.shape["sect"])
        body = shards if fits(*sizes) else general_shards
        return body(features, *others)

    return jax.shard_map(
        chosen, mesh=mesh, in_specs=in_specs, out_specs=out_specs, check_vma=False
    )
```

```python
import functools

import jax
import jax.numpy as jnp
from jax import lax
from jax.experimental import pallas as pl
from jax.experimental.pallas import tpu as pltpu
from jax.sharding import PartitionSpec as P

DILATIONS = (12, 24, 36)
PADDING = 36
PRECISE = lax.Precision.HIGHEST
ROW_BLOCK = 6
MOST_LAND = 4
VMEM_LIMIT = 32 * 2 ** 20
WHOLE_VMEM = 58 * 2 ** 20
POOL_ROWS = 8
F32 = jnp.float32
BF16 = jnp.bfloat16
VMEM = pl.BlockSpec(memory_space=pltpu.VMEM)
HBM = pl.BlockSpec(memory_space=pltpu.HBM)


def call(body, outs, in_specs, scratch, limit=VMEM_LIMIT):
    return pl.pallas_call(
        body,
        out_shape=outs,
        in_specs=in_specs,
        out_specs=jax.tree.map(lambda _: VMEM, outs),
        scratch_shapes=scratch,
        compiler_params=pltpu.CompilerParams(vmem_limit_bytes=limit),
        cost_estimate=pl.CostEstimate(flops=1024, bytes_accessed=1024, transcendentals=0),
    )


def reversed_bits(value, bits):
    return sum(((value >> bit) & 1) << (bits - 1 - bit) for bit in range(bits))


def fill_slots(mask_ref, slots_ref, batches, row_count):
    for image in range(batches):
        inner = range(1, row_count - 1)
        lives = {row: (mask_ref[image, row] > 0).astype(jnp.int32) for row in inner}
        land_total = sum(lives.values())
        land_before, sea_before = 0, 0
        chosen = [0] * (MOST_LAND - 2)
        for row in inner:
            live = lives[row]
            rank = jnp.where(live > 0, land_before, land_total + sea_before)
            chosen = [
                value + row * (rank == slot).astype(jnp.int32)
                for slot, value in enumerate(chosen)
            ]
            land_before = land_before + live
            sea_before = sea_before + (1 - live)
        base = image * MOST_LAND
        rows = [jnp.int32(0), *chosen, jnp.int32(row_count - 1)]
        flags = [(land_total > slot).astype(jnp.int32) for slot in range(MOST_LAND - 2)]
        flags = [mask_ref[image, 0], *flags, mask_ref[image, row_count - 1]]
        for slot in range(MOST_LAND):
            slots_ref[0, base + slot] = rows[slot]
            slots_ref[1, base + slot] = flags[slot]


def split_three(value):
    high = value.astype(BF16)
    rest = value - high.astype(F32)
    middle = rest.astype(BF16)
    low = (rest - middle.astype(F32)).astype(BF16)
    return high, middle, low


def precise_dot(value, weight):
    return sum(jnp.dot(part, weight, preferred_element_type=F32) for part in split_three(value))


def shifted(value, by, columns):
    blocks = value.reshape(-1, columns, value.shape[1])
    empty = jnp.zeros((blocks.shape[0], abs(by), value.shape[1]), value.dtype)
    if by > 0:
        moved = jnp.concatenate([empty, blocks[:, : columns - by]], axis=1)
    else:
        moved = jnp.concatenate([blocks[:, -by:], empty], axis=1)
    return moved.reshape(value.shape)


class Plan:
    def __init__(self, batches, row_count, columns, bands, sects):
        self.batches, self.row_count, self.columns = batches, row_count, columns
        self.bands, self.sects = bands, sects
        self.bits = sects.bit_length() - 1
        self.share_rows = batches * MOST_LAND // sects
        self.share = self.share_rows * columns
        self.terms = []
        for branch, dilation in enumerate(DILATIONS):
            hop = dilation // row_count
            if hop >= bands:
                continue
            up = [(b, b + hop) for b in range(bands - hop)]
            down = [(target, source) for source, target in up]
            if 2 * hop >= bands:
                self.terms.append((branch, hop, None, up + down))
            else:
                self.terms.append((branch, hop, 0, up))
                self.terms.append((branch, hop, 2, down))

    def rows_of(self, position, sect, slots_ref):
        owner = sect ^ reversed_bits(position, self.bits)
        for row in range(self.share_rows):
            place = owner * self.share_rows + row
            start = (position * self.share_rows + row) * self.columns
            yield lax.div(place, MOST_LAND), slots_ref[0, place], start


def tap_sum(rows, taps, dilation, columns):
    width = taps.shape[1] // 3
    if dilation >= columns:
        return jnp.dot(rows, taps[:, width : 2 * width], preferred_element_type=F32)
    result = jnp.dot(rows, taps, preferred_element_type=F32)
    return (
        result[:, width : 2 * width]
        + shifted(result[:, :width], dilation, columns)
        + shifted(result[:, 2 * width :], -dilation, columns)
    )


def store_halves(keep, send, index, value):
    half, width = keep.shape[0], value.shape[1]
    value = value.astype(BF16)
    keep[:, pl.ds(index * width, width)] = value[:half]
    send[:, pl.ds(index * width, width)] = value[half:]


def gather(plan, mask, features_ref, slots_ref, rows_ref):
    fill_slots(mask, slots_ref, plan.batches, plan.row_count)
    sect = lax.axis_index("sect")
    for position in range(plan.sects):
        for image, row, start in plan.rows_of(position, sect, slots_ref):
            rows_ref[pl.ds(start, plan.columns)] = features_ref[image, row]


def parts_of(value):
    high, low, _ = split_three(value)
    return jnp.concatenate([high.astype(F32), low.astype(F32)], axis=0)


def joined_parts(rows):
    return rows[:POOL_ROWS].astype(F32) + rows[POOL_ROWS:].astype(F32)


def pool_kernel(features_ref, weight_ref, out_ref):
    batches, row_count, columns, channels = features_ref.shape
    row = lax.broadcasted_iota(jnp.int32, (POOL_ROWS, channels), 0)
    sums = jnp.zeros((POOL_ROWS, channels), F32)
    for image in range(batches):
        cells = features_ref[image].astype(F32).reshape(row_count * columns, channels)
        sums = jnp.where(row == image, jnp.sum(cells, axis=0, keepdims=True), sums)
    out_ref[...] = parts_of(precise_dot(sums, weight_ref[...])).astype(BF16)


def edge_kernel(plan, low_ref, keep_ref, moved_ref, far_ref, first_ref, second_ref):
    far = keep_ref[...].astype(F32) + moved_ref[...].astype(F32)
    far_ref[...] = far.astype(BF16)
    cells, width = plan.batches * plan.columns, low_ref.shape[3]
    first_ref[pl.ds(cells, 2 * POOL_ROWS)] = far[plan.share :, :width].astype(BF16)
    odd = lax.rem(lax.axis_index("band"), 2)
    last = plan.row_count - 1
    for image in range(plan.batches):
        rows = pl.ds(image * plan.columns, plan.columns)
        first_ref[rows] = low_ref[image, last - odd * last]
        second_ref[rows] = low_ref[image, odd * last]


def fetch_taps(dilated_ref, branch, row_tap, taps_ref, index, sems):
    width = dilated_ref.shape[4]
    copies = []
    for tap in range(3):
        copy = pltpu.make_async_copy(
            dilated_ref.at[branch, row_tap, tap],
            taps_ref.at[index, :, pl.ds(tap * width, width)],
            sems.at[index, tap],
        )
        copy.start()
        copies.append(copy)
    return copies


def own_kernel(plan, mask_ref, features_ref, one_ref, dilated_ref, keep, send, slots_ref, land_ref, held_ref, rows_ref, ones_ref, taps_ref, sems, tap_sems):
    copies = [
        pltpu.make_async_copy(mask_ref, land_ref, sems.at[0]),
        pltpu.make_async_copy(features_ref, held_ref, sems.at[1]),
        pltpu.make_async_copy(one_ref, ones_ref, sems.at[2]),
    ]
    for copy in copies:
        copy.start()
    tap_copies = [
        fetch_taps(dilated_ref, branch, 1, taps_ref, branch, tap_sems)
        for branch in range(len(DILATIONS))
    ]
    copies[0].wait()
    copies[1].wait()
    gather(plan, land_ref, held_ref, slots_ref, rows_ref)
    copies[2].wait()
    value = jnp.dot(rows_ref[...], ones_ref[...], preferred_element_type=F32)
    store_halves(keep, send, 0, value)
    for branch, waits in enumerate(tap_copies):
        for copy in waits:
            copy.wait()
        value = tap_sum(rows_ref[...], taps_ref[branch], DILATIONS[branch], plan.columns)
        store_halves(keep, send, branch + 1, value)


def own_partials(plan, mask, features, weight_one, weight_dilated):
    channels, width = weight_one.shape
    half = plan.sects // 2 * plan.share
    out = jax.ShapeDtypeStruct((half, (1 + len(DILATIONS)) * width), BF16)
    return call(
        functools.partial(own_kernel, plan),
        (out, out),
        [HBM, HBM, HBM, HBM],
        [
            pltpu.SMEM((2, plan.batches * MOST_LAND), jnp.int32),
            pltpu.SMEM(mask.shape, jnp.int32),
            pltpu.VMEM(features.shape, BF16),
            pltpu.VMEM((2 * half, channels), BF16),
            pltpu.VMEM((channels, width), BF16),
            pltpu.VMEM((len(DILATIONS), channels, 3 * width), BF16),
            pltpu.SemaphoreType.DMA((3,)),
            pltpu.SemaphoreType.DMA((len(DILATIONS), 3)),
        ],
        WHOLE_VMEM,
    )(mask, features, weight_one, weight_dilated)


def far_kernel(plan, far_mask_ref, pool_ref, features_ref, *refs):
    terms = len(plan.terms)
    taps_refs, (keep, send, slots_ref, rows_ref) = refs[:terms], refs[terms:]
    pooled = pool_ref[...]
    block = plan.share + 2 * POOL_ROWS
    for term, taps_ref in enumerate(taps_refs):
        width = taps_ref.shape[2]
        gather(plan, far_mask_ref.at[term], features_ref, slots_ref, rows_ref)
        taps = jnp.concatenate([taps_ref[tap] for tap in range(3)], axis=1)
        dilation = DILATIONS[plan.terms[term][0]]
        value = tap_sum(rows_ref[...], taps, dilation, plan.columns).astype(BF16)
        lanes = pl.ds(term * width, width)
        for position in range(plan.sects):
            out = keep if position < plan.sects // 2 else send
            start = position % (plan.sects // 2) * block
            share = value[position * plan.share : (position + 1) * plan.share]
            out[pl.ds(start, plan.share), lanes] = share
            out[pl.ds(start + plan.share, 2 * POOL_ROWS), lanes] = pooled


def far_partials(plan, far_mask, pool, features, taps):
    channels, width = taps[0].shape[1:]
    rows = plan.sects // 2 * (plan.share + 2 * POOL_ROWS)
    out = jax.ShapeDtypeStruct((rows, len(taps) * width), BF16)
    return call(
        functools.partial(far_kernel, plan),
        (out, out),
        [VMEM] * (3 + len(taps)),
        [
            pltpu.SMEM((2, plan.batches * MOST_LAND), jnp.int32),
            pltpu.VMEM((plan.sects * plan.share, channels), BF16),
        ],
    )(far_mask, pool, features, *taps)


def low_kernel(plan, low_ref, first_ref, second_ref, reduce_ref, bias_reduce_ref, merging_ref, bias_ref, out_ref, framed_ref):
    batches, row_count, columns, depth = low_ref.shape
    band, bands = lax.axis_index("band"), plan.bands
    reduced = reduce_ref.shape[1]
    wide = 3 * reduced
    even = lax.rem(band, 2) == 0
    copied = lax.broadcasted_iota(jnp.int32, (reduced, wide), 1) % reduced
    copies = (copied == lax.broadcasted_iota(jnp.int32, (reduced, wide), 0)).astype(F32).astype(BF16)
    weight = jnp.dot(reduce_ref[...], copies, preferred_element_type=F32).astype(BF16)
    bias = precise_dot(bias_reduce_ref[...], copies)

    def reduce(rows):
        value = jnp.dot(rows, weight, preferred_element_type=F32) + bias
        value = jnp.maximum(value, 0.0).astype(BF16).astype(F32)
        lane = lax.broadcasted_iota(jnp.int32, value.shape, 1)
        return jnp.where(
            lane < reduced,
            shifted(value, 1, columns),
            jnp.where(lane < 2 * reduced, value, shifted(value, -1, columns)),
        )

    framed_ref[:, 1 : row_count + 1] = (
        reduce(low_ref[...].reshape(-1, depth)).astype(BF16).reshape(batches, row_count, columns, wide)
    )
    first = reduce(first_ref[: batches * columns])
    second = reduce(second_ref[...])
    above = jnp.where(even, second, first) * jnp.where(band > 0, 1.0, 0.0)
    below = jnp.where(even, first, second) * jnp.where(band < bands - 1, 1.0, 0.0)
    framed_ref[:, 0] = above.astype(BF16).reshape(batches, columns, wide)
    framed_ref[:, row_count + 1] = below.astype(BF16).reshape(batches, columns, wide)
    width = merging_ref.shape[2] - reduced
    for image in range(batches):
        total = jnp.zeros((row_count * columns, out_ref.shape[3]), F32) + bias_ref[...]
        for tap in range(3):
            rows = framed_ref[image, tap : tap + row_count].reshape(-1, wide)
            taps = jnp.concatenate([merging_ref[tap, side, width:] for side in range(3)], axis=0)
            total = total + jnp.dot(rows, taps, preferred_element_type=F32)
        out_ref[image] = total.reshape(row_count, columns, -1)


def project_kernel(plan, mask_ref, keep_ref, moved_ref, bias_branch_ref, pool_ref, bias_pool_ref, weight_ref, bias_ref, *refs):
    far_refs = refs[: len(plan.terms)]
    out_ref, edge_ref, slots_ref, context_ref = refs[len(plan.terms) :]
    columns, width = plan.columns, weight_ref.shape[1]
    sect = lax.axis_index("sect")
    fill_slots(mask_ref, slots_ref, plan.batches, plan.row_count)
    cells = plan.row_count * plan.bands * columns
    pooled = pool_ref[...] / cells
    pooled = jnp.maximum(pooled + bias_pool_ref[...], 0.0)
    context_ref[...] = precise_dot(pooled, weight_ref[4 * width :]) + bias_ref[...]
    total = jnp.zeros((plan.share, width), F32)
    for branch in range(4):
        lanes = pl.ds(branch * width, width)
        value = keep_ref[:, lanes].astype(F32) + moved_ref[:, lanes].astype(F32)
        for term, far in zip(plan.terms, far_refs):
            if term[0] + 1 == branch:
                value = value + far[: plan.share].astype(F32)
        value = jnp.maximum(value + bias_branch_ref[pl.ds(branch, 1)], 0.0).astype(BF16)
        total = total + jnp.dot(
            value, weight_ref[pl.ds(branch * width, width)], preferred_element_type=F32
        )
    for row in range(plan.share_rows):
        place = sect * plan.share_rows + row
        image = lax.div(place, MOST_LAND)
        keep = slots_ref[1, place].astype(F32)
        value = total[row * columns : (row + 1) * columns] + context_ref[pl.ds(image, 1)]
        out_ref[pl.ds(row * columns, columns)] = (jnp.maximum(value, 0.0) * keep).astype(BF16)
    at_top = lax.rem(sect * plan.share_rows, MOST_LAND) == 0

    @pl.when(at_top)
    def _():
        edge_ref[...] = out_ref[pl.ds(0, columns)]

    @pl.when(jnp.logical_not(at_top))
    def _():
        edge_ref[...] = out_ref[pl.ds(plan.share - columns, columns)]


def merge_kernel(plan, mask_ref, low_ref, weight_ref, *refs):
    sects, columns = plan.sects, plan.columns
    share_refs, edge_refs = refs[:sects], refs[sects : 2 * sects]
    out_ref, slots_ref, rows_ref, halo_ref, total_ref = refs[2 * sects :]
    width = weight_ref.shape[3]
    sect = lax.axis_index("sect")
    fill_slots(mask_ref, slots_ref, plan.batches, plan.row_count)

    def spread(value):
        wide = value.astype(F32)
        return (
            shifted(wide, 1, columns).astype(BF16),
            value,
            shifted(wide, -1, columns).astype(BF16),
        )

    def weight(tap):
        return jnp.concatenate([weight_ref[tap, side, :width] for side in range(3)], axis=0)

    total_ref[:, 1 : plan.row_count + 1] = low_ref[...]
    tops, bottoms = [], []
    for offset in range(sects):
        for side, value in enumerate(spread(share_refs[offset][...])):
            rows_ref[pl.ds(offset * plan.share, plan.share), pl.ds(side * width, width)] = value
        for side, value in enumerate(spread(edge_refs[offset][...])):
            halo_ref[pl.ds(offset * columns, columns), pl.ds(side * width, width)] = value
    for tap in range(3):
        taps = weight(tap)
        result = jnp.dot(rows_ref[...], taps, preferred_element_type=F32)
        if tap != 1:
            halo = jnp.dot(halo_ref[...], taps, preferred_element_type=F32)
        for offset in range(sects):
            owner = sect ^ offset
            for row in range(plan.share_rows):
                place = owner * plan.share_rows + row
                image = lax.div(place, MOST_LAND)
                at = slots_ref[0, place] + 2 - tap
                start = (offset * plan.share_rows + row) * columns
                total_ref[image, at] = total_ref[image, at] + result[start : start + columns]
            first = owner * plan.share_rows
            image = lax.div(first, MOST_LAND)
            top = lax.rem(first, MOST_LAND) == 0
            bottom = lax.rem(first + plan.share_rows, MOST_LAND) == 0
            if tap != 1:
                piece = halo[offset * columns : (offset + 1) * columns]
                at = 1 if tap == 0 else plan.row_count
                factor = jnp.where(top if tap == 0 else bottom, 1.0, 0.0)
                total_ref[image, at] = total_ref[image, at] + piece * factor
    for image in range(plan.batches):
        for row in range(plan.row_count):
            keep = mask_ref[image, row].astype(F32)
            out_ref[image, row] = (jnp.maximum(total_ref[image, row + 1], 0.0) * keep).astype(BF16)


def swap(value, axis, pattern):
    count = lax.axis_size(axis)
    return lax.ppermute(value, axis, [(i, i ^ pattern) for i in range(count)])


def add_halves(keep, moved):
    total = (keep.astype(F32) + moved.astype(F32)).astype(BF16)
    half = total.shape[0] // 2
    return total[:half], total[half:]


def spread_over(value, plan):
    values = {0: value}
    for bit in reversed(range(plan.bits)):
        for offset in list(values):
            values[offset ^ 1 << bit] = swap(values[offset], "sect", 1 << bit)
    return [values[offset] for offset in range(plan.sects)]


def swap_edges(edge, plan):
    pairs = []
    for image in range(plan.batches):
        top = image * MOST_LAND // plan.share_rows
        bottom = (image * MOST_LAND + MOST_LAND - 1) // plan.share_rows
        for band in range(plan.bands - 1):
            upper = band * plan.sects + bottom
            lower = (band + 1) * plan.sects + top
            pairs += [(upper, lower), (lower, upper)]
    return lax.ppermute(edge, ("band", "sect"), pairs)


def swap_low_edges(first, second, bands):
    first_pairs = [(b, b ^ 1) for b in range(bands)]
    second_pairs = []
    for b in range(1, bands - 1, 2):
        second_pairs += [(b, b + 1), (b + 1, b)]
    return lax.ppermute(first, "band", first_pairs), lax.ppermute(second, "band", second_pairs)


def fits(batches, row_count, columns, bands, sects, low_depth, width):
    slots = batches * MOST_LAND
    return (
        row_count == ROW_BLOCK
        and all(dilation % row_count == 0 for dilation in DILATIONS)
        and sects > 1
        and sects & (sects - 1) == 0
        and bands > min(DILATIONS) // row_count
        and low_depth == width
        and bands & (bands - 1) == 0
        and slots % sects == 0
        and MOST_LAND % (2 * (slots // sects)) == 0
        and columns % 16 == 0
        and batches <= POOL_ROWS
    )


def shards(
    features,
    low_level,
    land_mask,
    weight_one,
    weight_dilated,
    bias_branch,
    weight_pool,
    bias_pool,
    weight_project,
    bias_project,
    weight_reduce,
    bias_reduce,
    weight_merging,
    bias_merging,
):
    batches, row_count, columns, channels = features.shape
    bands, sects = lax.axis_size("band"), lax.axis_size("sect")
    plan = Plan(batches, row_count, columns, bands, sects)
    width = weight_one.shape[1]
    band = lax.axis_index("band")
    keep, send = own_partials(plan, land_mask, features, weight_one, weight_dilated)
    keep, send, late_mask, late_features, late_low = lax.optimization_barrier(
        (keep, send, land_mask, features, low_level)
    )
    far_masks = [
        lax.ppermute(late_mask, "band", [(target, source) for source, target in pairs])
        for _, _, _, pairs in plan.terms
    ]
    pool = call(
        pool_kernel, jax.ShapeDtypeStruct((2 * POOL_ROWS, width), BF16), [VMEM, VMEM], []
    )(late_features, weight_pool)
    moved = swap(send, "sect", 1)
    for bit in range(1, plan.bits - 1):
        keep, send = add_halves(keep, moved)
        moved = swap(send, "sect", 1 << bit)
    keep, send = add_halves(keep, moved)
    moved = swap(send, "sect", plan.sects // 2)
    far_mask = jnp.stack(far_masks)
    far_mask, send = lax.optimization_barrier((far_mask, send))
    taps = []
    for branch, hop, row_tap, _ in plan.terms:
        if row_tap is None:
            row_tap = jnp.where(band + hop < bands, 0, 2)
        start = (branch, row_tap, 0, 0, 0)
        size = (1, 1) + weight_dilated.shape[2:]
        taps.append(lax.dynamic_slice(weight_dilated, start, size)[0, 0])
    far_keep, far_send = far_partials(plan, far_mask, pool, late_features, taps)
    for bit in range(plan.bits - 1):
        far_moved = swap(far_send, "sect", 1 << bit)
        far_keep, far_send = add_halves(far_keep, far_moved)
    far_moved = swap(far_send, "sect", plan.sects // 2)
    far, first, second = call(
        functools.partial(edge_kernel, plan),
        (
            jax.ShapeDtypeStruct(far_keep.shape, BF16),
            jax.ShapeDtypeStruct((batches * columns + 2 * POOL_ROWS, width), BF16),
            jax.ShapeDtypeStruct((batches * columns, width), BF16),
        ),
        [VMEM] * 3,
        [],
    )(late_low, far_keep, far_moved)
    far_terms = []
    for term, (_, hop, _, pairs) in enumerate(plan.terms):
        rows = far if 2 * hop == bands else far[: plan.share]
        lanes = slice(term * width, (term + 1) * width)
        far_terms.append(lax.ppermute(rows[:, lanes], "band", pairs))
    own_pool = far[plan.share :, :width]
    first, second = swap_low_edges(first, second, bands)
    pool = joined_parts(own_pool) + joined_parts(first[batches * columns :])
    if bands == 4 and any(2 * term[1] == bands for term in plan.terms):
        halves = [term for term, entry in enumerate(plan.terms) if 2 * entry[1] == bands]
        pool = pool + joined_parts(far_terms[halves[0]][plan.share :])
        pool = pool + joined_parts(swap(own_pool, "band", 3))
    else:
        for bit in range(1, bands.bit_length() - 1):
            pool = pool + swap(pool, "band", 1 << bit)
    reduced = weight_reduce.shape[1]
    low_part = call(
        functools.partial(low_kernel, plan),
        jax.ShapeDtypeStruct((batches, row_count, columns, weight_merging.shape[3]), F32),
        [VMEM] * 7,
        [pltpu.VMEM((batches, row_count + 2, columns, 3 * reduced), BF16)],
    )(
        late_low,
        first,
        second,
        weight_reduce,
        bias_reduce[None],
        weight_merging,
        bias_merging[None],
    )
    keep, low_part = lax.optimization_barrier((keep, low_part))
    share = jax.ShapeDtypeStruct((plan.share, width), BF16)
    row = jax.ShapeDtypeStruct((columns, width), BF16)
    out, edge = call(
        functools.partial(project_kernel, plan),
        (share, row),
        [VMEM] * (8 + len(plan.terms)),
        [pltpu.SMEM((2, batches * MOST_LAND), jnp.int32), pltpu.VMEM((8, width), F32)],
    )(
        land_mask,
        keep,
        moved,
        bias_branch,
        pool,
        bias_pool[None],
        weight_project,
        bias_project[None],
        *far_terms,
    )
    halo = swap_edges(edge, plan)
    shares, halos = spread_over(out, plan), spread_over(halo, plan)
    live = batches * MOST_LAND * columns
    return call(
        functools.partial(merge_kernel, plan),
        jax.ShapeDtypeStruct(low_part.shape, BF16),
        [VMEM] * (3 + 2 * sects),
        [
            pltpu.SMEM((2, batches * MOST_LAND), jnp.int32),
            pltpu.VMEM((live, 3 * width), BF16),
            pltpu.VMEM((sects * columns, 3 * width), BF16),
            pltpu.VMEM((batches, row_count + 2, columns, width), F32),
        ],
    )(land_mask, low_part, weight_merging, *shares, *halos)


def from_behind(value, axis, by):
    count = lax.axis_size(axis)
    pairs = [(i, i + by) for i in range(count) if 0 <= i + by < count]
    return lax.ppermute(value, axis, pairs)


def extended(block, sides, width):
    for axis, dim in sides:
        count = lax.axis_size(axis)
        forward = [(i, i + 1) for i in range(count - 1)]
        backward = [(target, source) for source, target in forward]
        low = lax.ppermute(
            lax.slice_in_dim(block, block.shape[dim] - width, None, axis=dim), axis, forward
        )
        high = lax.ppermute(lax.slice_in_dim(block, 0, width, axis=dim), axis, backward)
        block = jnp.concatenate([low, block, high], axis=dim)
    return block


def extend_rows(features):
    row_count = features.shape[1]
    reach_bands = min((PADDING + row_count - 1) // row_count, lax.axis_size("band") - 1)
    upper_blocks = []
    lower_blocks = []
    moving_up = features
    moving_down = features
    for hop_index in range(reach_bands):
        moving_up = from_behind(moving_up, "band", 1)
        moving_down = from_behind(moving_down, "band", -1)
        upper_blocks.insert(0, moving_up)
        lower_blocks.append(moving_down)
    margin = reach_bands * row_count
    stacked = jnp.concatenate(upper_blocks + [features] + lower_blocks, axis=1)
    if margin >= PADDING:
        stacked = stacked[:, margin - PADDING : margin + row_count + PADDING]
    else:
        stacked = jnp.pad(stacked, ((0, 0), (PADDING - margin, PADDING - margin), (0, 0), (0, 0)))
    return jnp.pad(stacked, ((0, 0), (0, 0), (PADDING, PADDING), (0, 0)))


def branch_terms(window, select_rows, weight_one, weight_dilated, live_rows, col_count):
    batches = window.shape[0]
    channels = window.shape[3]
    centre = select_rows(0)[:, :, PADDING : PADDING + col_count].reshape(-1, channels)
    partials = [jnp.dot(centre, weight_one, preferred_element_type=jnp.float32)]
    for branch_index, dilation in enumerate(DILATIONS):
        running = jnp.zeros((centre.shape[0], weight_one.shape[1]), jnp.float32)
        for row_tap in range(3):
            band_rows = select_rows(dilation * (row_tap - 1))
            for col_tap in range(3):
                left = PADDING + dilation * (col_tap - 1)
                tap_rows = band_rows[:, :, left : left + col_count].reshape(-1, channels)
                running = running + jnp.dot(
                    tap_rows,
                    weight_dilated[branch_index, row_tap, col_tap],
                    preferred_element_type=jnp.float32,
                )
        partials.append(running)
    return jnp.concatenate(partials, axis=1).reshape(batches, live_rows, col_count, -1)


def pool_context(features, weight_pool, bias_pool, row_count, col_count):
    local_sum = jnp.sum(features, axis=(1, 2), dtype=jnp.float32)
    cell_count = row_count * lax.axis_size("band") * col_count
    weight_full = weight_pool.astype(jnp.float32)
    average = lax.psum(local_sum, "band") / cell_count
    pre_relu = lax.psum(jnp.dot(average, weight_full, precision=PRECISE), "sect")
    return jax.nn.relu(pre_relu + bias_pool)


def general_shards(
    features,
    low_level,
    land_mask,
    weight_one,
    weight_dilated,
    bias_branch,
    weight_pool,
    bias_pool,
    weight_project,
    bias_project,
    weight_reduce,
    bias_reduce,
    weight_merging,
    bias_merging,
):
    batches, row_count, col_count, channels = features.shape
    branch_width = weight_project.shape[1]
    window = extend_rows(features)
    pooled = pool_context(features, weight_pool, bias_pool, row_count, col_count)
    context = jnp.dot(
        pooled, weight_project[4 * branch_width :].astype(jnp.float32), precision=PRECISE
    )
    row_mask = land_mask.astype(jnp.float32)

    def select_rows(offset):
        return window[:, PADDING + offset : PADDING + offset + row_count]

    partials = branch_terms(window, select_rows, weight_one, weight_dilated, row_count, col_count)
    flat_terms = partials.astype(jnp.bfloat16).reshape(-1, partials.shape[3])
    summed_cells = lax.psum_scatter(flat_terms, "sect", scatter_dimension=0, tiled=True).astype(
        jnp.float32
    )
    share_cells = summed_cells.shape[0]
    first_cell = lax.axis_index("sect") * share_cells
    branch_cells = jax.nn.relu(summed_cells + bias_branch.reshape(-1)).astype(jnp.bfloat16)
    projected_cells = jnp.dot(
        branch_cells, weight_project[: 4 * branch_width], preferred_element_type=jnp.float32
    )
    cell_ids = first_cell + lax.broadcasted_iota(jnp.int32, (share_cells,), 0)
    batch_of = cell_ids // (row_count * col_count)
    batch_onehot = (batch_of[:, None] == lax.broadcasted_iota(jnp.int32, (1, batches), 1)).astype(
        jnp.float32
    )
    context_cells = jnp.dot(batch_onehot, context, precision=PRECISE)
    keep_all = jnp.broadcast_to(row_mask[:, :, None], (batches, row_count, col_count)).reshape(-1)
    keep_cells = lax.dynamic_slice_in_dim(keep_all, first_cell, share_cells, 0)
    out_cells = (
        jax.nn.relu(projected_cells + context_cells + bias_project) * keep_cells[:, None]
    ).astype(jnp.bfloat16)
    project_out = lax.all_gather(out_cells, "sect", axis=0, tiled=True).reshape(
        batches, row_count, col_count, branch_width
    )
    low_reduced = (
        jax.nn.relu(
            jnp.dot(
                low_level.reshape(-1, low_level.shape[3]),
                weight_reduce,
                preferred_element_type=jnp.float32,
            )
            + bias_reduce
        )
        .astype(jnp.bfloat16)
        .reshape(batches, row_count, col_count, -1)
    )
    joined = jnp.concatenate([project_out, low_reduced], axis=3)
    framed = extended(joined, (("band", 1),), 1)
    framed = jnp.pad(framed, ((0, 0), (0, 0), (1, 1), (0, 0)))
    running = jnp.zeros((batches * row_count * col_count, weight_merging.shape[3]), jnp.float32)
    for row_tap in range(3):
        for col_tap in range(3):
            tap_rows = framed[
                :, row_tap : row_tap + row_count, col_tap : col_tap + col_count
            ].reshape(-1, joined.shape[3])
            running = running + jnp.dot(
                tap_rows, weight_merging[row_tap, col_tap], preferred_element_type=jnp.float32
            )
    merged_map = (
        jax.nn.relu(running + bias_merging).reshape(batches, row_count, col_count, -1)
        * row_mask[:, :, None, None]
    )
    return merged_map.astype(jnp.bfloat16)


def solution(mesh):
    in_specs = (
        P("grp", "band", None, "sect"),
        P("grp", "band", None, None),
        P("grp", "band"),
        P("sect", None),
        P(None, None, None, "sect", None),
        P(),
        P("sect", None),
        P(),
        P(),
        P(),
        P(),
        P(),
        P(),
        P(),
    )
    out_specs = P("grp", "band", None, None)

    def chosen(features, low_level, land_mask, weight_one, *others):
        batches, row_count, columns, _ = features.shape
        depths = (low_level.shape[3], weight_one.shape[1])
        sizes = (batches, row_count, columns, mesh.shape["band"], mesh.shape["sect"])
        body = shards if fits(*sizes, *depths) else general_shards
        return body(features, low_level, land_mask, weight_one, *others)

    return jax.shard_map(
        chosen, mesh=mesh, in_specs=in_specs, out_specs=out_specs, check_vma=False
    )
```

```python
import functools

import jax
import jax.numpy as jnp
from jax import lax
from jax.experimental import pallas as pl
from jax.experimental.pallas import tpu as pltpu
from jax.sharding import PartitionSpec as P

DILATIONS = (12, 24, 36)
PADDING = 36
PRECISE = lax.Precision.HIGHEST
ROW_BLOCK = 6
MOST_LAND = 4
VMEM_LIMIT = 32 * 2 ** 20
WHOLE_VMEM = 58 * 2 ** 20
POOL_ROWS = 8
F32 = jnp.float32
BF16 = jnp.bfloat16
VMEM = pl.BlockSpec(memory_space=pltpu.VMEM)
HBM = pl.BlockSpec(memory_space=pltpu.HBM)


def call(body, outs, in_specs, scratch, limit=VMEM_LIMIT):
    return pl.pallas_call(
        body,
        out_shape=outs,
        in_specs=in_specs,
        out_specs=jax.tree.map(lambda _: VMEM, outs),
        scratch_shapes=scratch,
        compiler_params=pltpu.CompilerParams(vmem_limit_bytes=limit),
        cost_estimate=pl.CostEstimate(flops=1024, bytes_accessed=1024, transcendentals=0),
    )


def reversed_bits(value, bits):
    return sum(((value >> bit) & 1) << (bits - 1 - bit) for bit in range(bits))


def fill_slots(mask_ref, slots_ref, batches, row_count):
    for image in range(batches):
        inner = range(1, row_count - 1)
        lives = {row: (mask_ref[image, row] > 0).astype(jnp.int32) for row in inner}
        land_total = sum(lives.values())
        land_before, sea_before = 0, 0
        chosen = [0] * (MOST_LAND - 2)
        for row in inner:
            live = lives[row]
            rank = jnp.where(live > 0, land_before, land_total + sea_before)
            chosen = [
                value + row * (rank == slot).astype(jnp.int32)
                for slot, value in enumerate(chosen)
            ]
            land_before = land_before + live
            sea_before = sea_before + (1 - live)
        base = image * MOST_LAND
        rows = [jnp.int32(0), *chosen, jnp.int32(row_count - 1)]
        flags = [(land_total > slot).astype(jnp.int32) for slot in range(MOST_LAND - 2)]
        flags = [mask_ref[image, 0], *flags, mask_ref[image, row_count - 1]]
        for slot in range(MOST_LAND):
            slots_ref[0, base + slot] = rows[slot]
            slots_ref[1, base + slot] = flags[slot]


def split_three(value):
    high = value.astype(BF16)
    rest = value - high.astype(F32)
    middle = rest.astype(BF16)
    low = (rest - middle.astype(F32)).astype(BF16)
    return high, middle, low


def precise_dot(value, weight):
    return sum(jnp.dot(part, weight, preferred_element_type=F32) for part in split_three(value))


def shifted(value, by, columns):
    blocks = value.reshape(-1, columns, value.shape[1])
    empty = jnp.zeros((blocks.shape[0], abs(by), value.shape[1]), value.dtype)
    if by > 0:
        moved = jnp.concatenate([empty, blocks[:, : columns - by]], axis=1)
    else:
        moved = jnp.concatenate([blocks[:, -by:], empty], axis=1)
    return moved.reshape(value.shape)


class Plan:
    def __init__(self, batches, row_count, columns, bands, sects):
        self.batches, self.row_count, self.columns = batches, row_count, columns
        self.bands, self.sects = bands, sects
        self.bits = sects.bit_length() - 1
        self.share_rows = batches * MOST_LAND // sects
        self.share = self.share_rows * columns
        self.terms = []
        for branch, dilation in enumerate(DILATIONS):
            hop = dilation // row_count
            if hop >= bands:
                continue
            up = [(b, b + hop) for b in range(bands - hop)]
            down = [(target, source) for source, target in up]
            if 2 * hop >= bands:
                self.terms.append((branch, hop, None, up + down))
            else:
                self.terms.append((branch, hop, 0, up))
                self.terms.append((branch, hop, 2, down))

    def rows_of(self, position, sect, slots_ref):
        owner = sect ^ reversed_bits(position, self.bits)
        for row in range(self.share_rows):
            place = owner * self.share_rows + row
            start = (position * self.share_rows + row) * self.columns
            yield lax.div(place, MOST_LAND), slots_ref[0, place], start


def tap_sum(rows, taps, dilation, columns):
    width = taps.shape[1] // 3
    if dilation >= columns:
        return jnp.dot(rows, taps[:, width : 2 * width], preferred_element_type=F32)
    result = jnp.dot(rows, taps, preferred_element_type=F32)
    return (
        result[:, width : 2 * width]
        + shifted(result[:, :width], dilation, columns)
        + shifted(result[:, 2 * width :], -dilation, columns)
    )


def store_halves(keep, send, index, value):
    half, width = keep.shape[0], value.shape[1]
    value = value.astype(BF16)
    keep[:, pl.ds(index * width, width)] = value[:half]
    send[:, pl.ds(index * width, width)] = value[half:]


def gather(plan, mask, features_ref, slots_ref, rows_ref):
    fill_slots(mask, slots_ref, plan.batches, plan.row_count)
    sect = lax.axis_index("sect")
    for position in range(plan.sects):
        for image, row, start in plan.rows_of(position, sect, slots_ref):
            rows_ref[pl.ds(start, plan.columns)] = features_ref[image, row]


def parts_of(value):
    high, low, _ = split_three(value)
    return jnp.concatenate([high.astype(F32), low.astype(F32)], axis=0)


def joined_parts(rows):
    return rows[:POOL_ROWS].astype(F32) + rows[POOL_ROWS:].astype(F32)


def pool_kernel(features_ref, weight_ref, out_ref):
    batches, row_count, columns, channels = features_ref.shape
    row = lax.broadcasted_iota(jnp.int32, (POOL_ROWS, channels), 0)
    sums = jnp.zeros((POOL_ROWS, channels), F32)
    for image in range(batches):
        cells = features_ref[image].astype(F32).reshape(row_count * columns, channels)
        sums = jnp.where(row == image, jnp.sum(cells, axis=0, keepdims=True), sums)
    out_ref[...] = parts_of(precise_dot(sums, weight_ref[...])).astype(BF16)


def copy_edges(plan, low_ref, out_ref, parity):
    upper = lax.rem(lax.axis_index("band") + parity, 2) == 0
    row = jnp.where(upper, plan.row_count - 1, 0)
    for image in range(plan.batches):
        out_ref[pl.ds(image * plan.columns, plan.columns)] = low_ref[image, row]


def second_edge_kernel(plan, low_ref, out_ref):
    copy_edges(plan, low_ref, out_ref, 1)


def edge_kernel(plan, low_ref, keep_ref, moved_ref, far_ref, first_ref):
    far = keep_ref[...].astype(F32) + moved_ref[...].astype(F32)
    far_ref[...] = far.astype(BF16)
    cells, width = plan.batches * plan.columns, low_ref.shape[3]
    first_ref[pl.ds(cells, 2 * POOL_ROWS)] = far[plan.share :, :width].astype(BF16)
    copy_edges(plan, low_ref, first_ref, 0)


def fetch_taps(dilated_ref, branch, row_tap, taps_ref, index, sems):
    width = dilated_ref.shape[4]
    copies = []
    for tap in range(3):
        copy = pltpu.make_async_copy(
            dilated_ref.at[branch, row_tap, tap],
            taps_ref.at[index, :, pl.ds(tap * width, width)],
            sems.at[index, tap],
        )
        copy.start()
        copies.append(copy)
    return copies


def own_kernel(plan, mask_ref, features_ref, one_ref, dilated_ref, keep, send, slots_ref, land_ref, held_ref, rows_ref, ones_ref, taps_ref, sems, tap_sems):
    copies = [
        pltpu.make_async_copy(mask_ref, land_ref, sems.at[0]),
        pltpu.make_async_copy(features_ref, held_ref, sems.at[1]),
        pltpu.make_async_copy(one_ref, ones_ref, sems.at[2]),
    ]
    for copy in copies:
        copy.start()
    tap_copies = [
        fetch_taps(dilated_ref, branch, 1, taps_ref, branch, tap_sems)
        for branch in range(len(DILATIONS))
    ]
    copies[0].wait()
    copies[1].wait()
    gather(plan, land_ref, held_ref, slots_ref, rows_ref)
    copies[2].wait()
    value = jnp.dot(rows_ref[...], ones_ref[...], preferred_element_type=F32)
    store_halves(keep, send, 0, value)
    for branch, waits in enumerate(tap_copies):
        for copy in waits:
            copy.wait()
        value = tap_sum(rows_ref[...], taps_ref[branch], DILATIONS[branch], plan.columns)
        store_halves(keep, send, branch + 1, value)


def own_partials(plan, mask, features, weight_one, weight_dilated):
    channels, width = weight_one.shape
    half = plan.sects // 2 * plan.share
    out = jax.ShapeDtypeStruct((half, (1 + len(DILATIONS)) * width), BF16)
    return call(
        functools.partial(own_kernel, plan),
        (out, out),
        [HBM, HBM, HBM, HBM],
        [
            pltpu.SMEM((2, plan.batches * MOST_LAND), jnp.int32),
            pltpu.SMEM(mask.shape, jnp.int32),
            pltpu.VMEM(features.shape, BF16),
            pltpu.VMEM((2 * half, channels), BF16),
            pltpu.VMEM((channels, width), BF16),
            pltpu.VMEM((len(DILATIONS), channels, 3 * width), BF16),
            pltpu.SemaphoreType.DMA((3,)),
            pltpu.SemaphoreType.DMA((len(DILATIONS), 3)),
        ],
        WHOLE_VMEM,
    )(mask, features, weight_one, weight_dilated)


def far_kernel(plan, far_mask_ref, pool_ref, features_ref, *refs):
    terms = len(plan.terms)
    taps_refs, (keep, send, slots_ref, rows_ref) = refs[:terms], refs[terms:]
    pooled = pool_ref[...]
    block = plan.share + 2 * POOL_ROWS
    for term, taps_ref in enumerate(taps_refs):
        width = taps_ref.shape[2]
        gather(plan, far_mask_ref.at[term], features_ref, slots_ref, rows_ref)
        taps = jnp.concatenate([taps_ref[tap] for tap in range(3)], axis=1)
        dilation = DILATIONS[plan.terms[term][0]]
        value = tap_sum(rows_ref[...], taps, dilation, plan.columns).astype(BF16)
        lanes = pl.ds(term * width, width)
        for position in range(plan.sects):
            out = keep if position < plan.sects // 2 else send
            start = position % (plan.sects // 2) * block
            share = value[position * plan.share : (position + 1) * plan.share]
            out[pl.ds(start, plan.share), lanes] = share
            out[pl.ds(start + plan.share, 2 * POOL_ROWS), lanes] = pooled


def far_partials(plan, far_mask, pool, features, taps):
    channels, width = taps[0].shape[1:]
    rows = plan.sects // 2 * (plan.share + 2 * POOL_ROWS)
    out = jax.ShapeDtypeStruct((rows, len(taps) * width), BF16)
    return call(
        functools.partial(far_kernel, plan),
        (out, out),
        [VMEM] * (3 + len(taps)),
        [
            pltpu.SMEM((2, plan.batches * MOST_LAND), jnp.int32),
            pltpu.VMEM((plan.sects * plan.share, channels), BF16),
        ],
    )(far_mask, pool, features, *taps)


def low_kernel(plan, low_ref, first_ref, second_ref, reduce_ref, bias_reduce_ref, merging_ref, bias_ref, out_ref, framed_ref):
    batches, row_count, columns, depth = low_ref.shape
    band, bands = lax.axis_index("band"), plan.bands
    reduced = reduce_ref.shape[1]
    wide = 3 * reduced
    even = lax.rem(band, 2) == 0
    copied = lax.broadcasted_iota(jnp.int32, (reduced, wide), 1) % reduced
    copies = (copied == lax.broadcasted_iota(jnp.int32, (reduced, wide), 0)).astype(F32).astype(BF16)
    weight = jnp.dot(reduce_ref[...], copies, preferred_element_type=F32).astype(BF16)
    bias = precise_dot(bias_reduce_ref[...], copies)

    def reduce(rows):
        value = jnp.dot(rows, weight, preferred_element_type=F32) + bias
        value = jnp.maximum(value, 0.0).astype(BF16).astype(F32)
        lane = lax.broadcasted_iota(jnp.int32, value.shape, 1)
        return jnp.where(
            lane < reduced,
            shifted(value, 1, columns),
            jnp.where(lane < 2 * reduced, value, shifted(value, -1, columns)),
        )

    framed_ref[:, 1 : row_count + 1] = (
        reduce(low_ref[...].reshape(-1, depth)).astype(BF16).reshape(batches, row_count, columns, wide)
    )
    first = reduce(first_ref[: batches * columns])
    second = reduce(second_ref[...])
    above = jnp.where(even, second, first) * jnp.where(band > 0, 1.0, 0.0)
    below = jnp.where(even, first, second) * jnp.where(band < bands - 1, 1.0, 0.0)
    framed_ref[:, 0] = above.astype(BF16).reshape(batches, columns, wide)
    framed_ref[:, row_count + 1] = below.astype(BF16).reshape(batches, columns, wide)
    width = merging_ref.shape[2] - reduced
    for image in range(batches):
        total = jnp.zeros((row_count * columns, out_ref.shape[3]), F32) + bias_ref[...]
        for tap in range(3):
            rows = framed_ref[image, tap : tap + row_count].reshape(-1, wide)
            taps = jnp.concatenate([merging_ref[tap, side, width:] for side in range(3)], axis=0)
            total = total + jnp.dot(rows, taps, preferred_element_type=F32)
        out_ref[image] = total.reshape(row_count, columns, -1)


def project_kernel(plan, mask_ref, keep_ref, moved_ref, bias_branch_ref, pool_ref, bias_pool_ref, weight_ref, bias_ref, *refs):
    far_refs = refs[: len(plan.terms)]
    out_ref, edge_ref, slots_ref, context_ref = refs[len(plan.terms) :]
    columns, width = plan.columns, weight_ref.shape[1]
    sect = lax.axis_index("sect")
    fill_slots(mask_ref, slots_ref, plan.batches, plan.row_count)
    cells = plan.row_count * plan.bands * columns
    pooled = pool_ref[...] / cells
    pooled = jnp.maximum(pooled + bias_pool_ref[...], 0.0)
    context_ref[...] = precise_dot(pooled, weight_ref[4 * width :]) + bias_ref[...]
    total = jnp.zeros((plan.share, width), F32)
    for branch in range(4):
        lanes = pl.ds(branch * width, width)
        value = keep_ref[:, lanes].astype(F32) + moved_ref[:, lanes].astype(F32)
        for term, far in zip(plan.terms, far_refs):
            if term[0] + 1 == branch:
                value = value + far[: plan.share].astype(F32)
        value = jnp.maximum(value + bias_branch_ref[pl.ds(branch, 1)], 0.0).astype(BF16)
        total = total + jnp.dot(
            value, weight_ref[pl.ds(branch * width, width)], preferred_element_type=F32
        )
    for row in range(plan.share_rows):
        place = sect * plan.share_rows + row
        image = lax.div(place, MOST_LAND)
        keep = slots_ref[1, place].astype(F32)
        value = total[row * columns : (row + 1) * columns] + context_ref[pl.ds(image, 1)]
        out_ref[pl.ds(row * columns, columns)] = (jnp.maximum(value, 0.0) * keep).astype(BF16)
    at_top = lax.rem(sect * plan.share_rows, MOST_LAND) == 0

    @pl.when(at_top)
    def _():
        edge_ref[...] = out_ref[pl.ds(0, columns)]

    @pl.when(jnp.logical_not(at_top))
    def _():
        edge_ref[...] = out_ref[pl.ds(plan.share - columns, columns)]


def merge_kernel(plan, mask_ref, low_ref, weight_ref, *refs):
    sects, columns = plan.sects, plan.columns
    share_refs, edge_refs = refs[:sects], refs[sects : 2 * sects]
    out_ref, slots_ref, rows_ref, halo_ref, total_ref = refs[2 * sects :]
    width = weight_ref.shape[3]
    sect = lax.axis_index("sect")
    fill_slots(mask_ref, slots_ref, plan.batches, plan.row_count)

    def spread(value):
        wide = value.astype(F32)
        return (
            shifted(wide, 1, columns).astype(BF16),
            value,
            shifted(wide, -1, columns).astype(BF16),
        )

    def weight(tap):
        return jnp.concatenate([weight_ref[tap, side, :width] for side in range(3)], axis=0)

    total_ref[:, 1 : plan.row_count + 1] = low_ref[...]
    tops, bottoms = [], []
    for offset in range(sects):
        for side, value in enumerate(spread(share_refs[offset][...])):
            rows_ref[pl.ds(offset * plan.share, plan.share), pl.ds(side * width, width)] = value
        for side, value in enumerate(spread(edge_refs[offset][...])):
            halo_ref[pl.ds(offset * columns, columns), pl.ds(side * width, width)] = value
    for tap in range(3):
        taps = weight(tap)
        result = jnp.dot(rows_ref[...], taps, preferred_element_type=F32)
        if tap != 1:
            halo = jnp.dot(halo_ref[...], taps, preferred_element_type=F32)
        for offset in range(sects):
            owner = sect ^ offset
            for row in range(plan.share_rows):
                place = owner * plan.share_rows + row
                image = lax.div(place, MOST_LAND)
                at = slots_ref[0, place] + 2 - tap
                start = (offset * plan.share_rows + row) * columns
                total_ref[image, at] = total_ref[image, at] + result[start : start + columns]
            first = owner * plan.share_rows
            image = lax.div(first, MOST_LAND)
            top = lax.rem(first, MOST_LAND) == 0
            bottom = lax.rem(first + plan.share_rows, MOST_LAND) == 0
            if tap != 1:
                piece = halo[offset * columns : (offset + 1) * columns]
                at = 1 if tap == 0 else plan.row_count
                factor = jnp.where(top if tap == 0 else bottom, 1.0, 0.0)
                total_ref[image, at] = total_ref[image, at] + piece * factor
    for image in range(plan.batches):
        for row in range(plan.row_count):
            keep = mask_ref[image, row].astype(F32)
            out_ref[image, row] = (jnp.maximum(total_ref[image, row + 1], 0.0) * keep).astype(BF16)


def swap(value, axis, pattern):
    count = lax.axis_size(axis)
    return lax.ppermute(value, axis, [(i, i ^ pattern) for i in range(count)])


def add_halves(keep, moved):
    total = (keep.astype(F32) + moved.astype(F32)).astype(BF16)
    half = total.shape[0] // 2
    return total[:half], total[half:]


def spread_over(value, plan):
    values = {0: value}
    for bit in reversed(range(plan.bits)):
        for offset in list(values):
            values[offset ^ 1 << bit] = swap(values[offset], "sect", 1 << bit)
    return [values[offset] for offset in range(plan.sects)]


def swap_edges(edge, plan):
    pairs = []
    for image in range(plan.batches):
        top = image * MOST_LAND // plan.share_rows
        bottom = (image * MOST_LAND + MOST_LAND - 1) // plan.share_rows
        for band in range(plan.bands - 1):
            upper = band * plan.sects + bottom
            lower = (band + 1) * plan.sects + top
            pairs += [(upper, lower), (lower, upper)]
    return lax.ppermute(edge, ("band", "sect"), pairs)


def border_pairs(bands):
    pairs = []
    for band in range(1, bands - 1, 2):
        pairs += [(band, band + 1), (band + 1, band)]
    return pairs


def fits(batches, row_count, columns, bands, sects, low_depth, width):
    slots = batches * MOST_LAND
    return (
        row_count == ROW_BLOCK
        and all(dilation % row_count == 0 for dilation in DILATIONS)
        and sects > 1
        and sects & (sects - 1) == 0
        and bands > min(DILATIONS) // row_count
        and low_depth == width
        and bands & (bands - 1) == 0
        and slots % sects == 0
        and MOST_LAND % (2 * (slots // sects)) == 0
        and columns % 16 == 0
        and batches <= POOL_ROWS
    )


def shards(
    features,
    low_level,
    land_mask,
    weight_one,
    weight_dilated,
    bias_branch,
    weight_pool,
    bias_pool,
    weight_project,
    bias_project,
    weight_reduce,
    bias_reduce,
    weight_merging,
    bias_merging,
):
    batches, row_count, columns, channels = features.shape
    bands, sects = lax.axis_size("band"), lax.axis_size("sect")
    plan = Plan(batches, row_count, columns, bands, sects)
    width = weight_one.shape[1]
    band = lax.axis_index("band")
    keep, send = own_partials(plan, land_mask, features, weight_one, weight_dilated)
    keep, send, late_mask, late_features, late_low = lax.optimization_barrier(
        (keep, send, land_mask, features, low_level)
    )
    far_masks = [
        lax.ppermute(late_mask, "band", [(target, source) for source, target in pairs])
        for _, _, _, pairs in plan.terms
    ]
    pool = call(
        pool_kernel, jax.ShapeDtypeStruct((2 * POOL_ROWS, width), BF16), [VMEM, VMEM], []
    )(late_features, weight_pool)
    moved = swap(send, "sect", 1)
    for bit in range(1, plan.bits - 1):
        keep, send = add_halves(keep, moved)
        moved = swap(send, "sect", 1 << bit)
    keep, send = add_halves(keep, moved)
    moved = swap(send, "sect", plan.sects // 2)
    far_mask = jnp.stack(far_masks)
    far_mask, send = lax.optimization_barrier((far_mask, send))
    taps = []
    for branch, hop, row_tap, _ in plan.terms:
        if row_tap is None:
            row_tap = jnp.where(band + hop < bands, 0, 2)
        start = (branch, row_tap, 0, 0, 0)
        size = (1, 1) + weight_dilated.shape[2:]
        taps.append(lax.dynamic_slice(weight_dilated, start, size)[0, 0])
    far_keep, far_send = far_partials(plan, far_mask, pool, late_features, taps)
    far_keep, far_send, late_low = lax.optimization_barrier((far_keep, far_send, late_low))
    for bit in range(plan.bits - 1):
        far_moved = swap(far_send, "sect", 1 << bit)
        far_keep, far_send = add_halves(far_keep, far_moved)
    far_moved = swap(far_send, "sect", plan.sects // 2)
    second = call(
        functools.partial(second_edge_kernel, plan),
        jax.ShapeDtypeStruct((batches * columns, width), BF16),
        [VMEM],
        [],
    )(late_low)
    second = lax.ppermute(second, "band", border_pairs(bands))
    far_moved, second = lax.optimization_barrier((far_moved, second))
    far, first = call(
        functools.partial(edge_kernel, plan),
        (
            jax.ShapeDtypeStruct(far_keep.shape, BF16),
            jax.ShapeDtypeStruct((batches * columns + 2 * POOL_ROWS, width), BF16),
        ),
        [VMEM] * 3,
        [],
    )(late_low, far_keep, far_moved)
    far_terms = []
    for term, (_, hop, _, pairs) in enumerate(plan.terms):
        rows = far if 2 * hop == bands else far[: plan.share]
        lanes = slice(term * width, (term + 1) * width)
        far_terms.append(lax.ppermute(rows[:, lanes], "band", pairs))
    own_pool = far[plan.share :, :width]
    first = swap(first, "band", 1)
    pool = joined_parts(own_pool) + joined_parts(first[batches * columns :])
    if bands == 4 and any(2 * term[1] == bands for term in plan.terms):
        halves = [term for term, entry in enumerate(plan.terms) if 2 * entry[1] == bands]
        pool = pool + joined_parts(far_terms[halves[0]][plan.share :])
        pool = pool + joined_parts(swap(own_pool, "band", 3))
    else:
        for bit in range(1, bands.bit_length() - 1):
            pool = pool + swap(pool, "band", 1 << bit)
    reduced = weight_reduce.shape[1]
    low_part = call(
        functools.partial(low_kernel, plan),
        jax.ShapeDtypeStruct((batches, row_count, columns, weight_merging.shape[3]), F32),
        [VMEM] * 7,
        [pltpu.VMEM((batches, row_count + 2, columns, 3 * reduced), BF16)],
    )(
        late_low,
        first,
        second,
        weight_reduce,
        bias_reduce[None],
        weight_merging,
        bias_merging[None],
    )
    keep, low_part = lax.optimization_barrier((keep, low_part))
    share = jax.ShapeDtypeStruct((plan.share, width), BF16)
    row = jax.ShapeDtypeStruct((columns, width), BF16)
    out, edge = call(
        functools.partial(project_kernel, plan),
        (share, row),
        [VMEM] * (8 + len(plan.terms)),
        [pltpu.SMEM((2, batches * MOST_LAND), jnp.int32), pltpu.VMEM((8, width), F32)],
    )(
        land_mask,
        keep,
        moved,
        bias_branch,
        pool,
        bias_pool[None],
        weight_project,
        bias_project[None],
        *far_terms,
    )
    halo = swap_edges(edge, plan)
    shares, halos = spread_over(out, plan), spread_over(halo, plan)
    live = batches * MOST_LAND * columns
    return call(
        functools.partial(merge_kernel, plan),
        jax.ShapeDtypeStruct(low_part.shape, BF16),
        [VMEM] * (3 + 2 * sects),
        [
            pltpu.SMEM((2, batches * MOST_LAND), jnp.int32),
            pltpu.VMEM((live, 3 * width), BF16),
            pltpu.VMEM((sects * columns, 3 * width), BF16),
            pltpu.VMEM((batches, row_count + 2, columns, width), F32),
        ],
    )(land_mask, low_part, weight_merging, *shares, *halos)


def from_behind(value, axis, by):
    count = lax.axis_size(axis)
    pairs = [(i, i + by) for i in range(count) if 0 <= i + by < count]
    return lax.ppermute(value, axis, pairs)


def extended(block, sides, width):
    for axis, dim in sides:
        count = lax.axis_size(axis)
        forward = [(i, i + 1) for i in range(count - 1)]
        backward = [(target, source) for source, target in forward]
        low = lax.ppermute(
            lax.slice_in_dim(block, block.shape[dim] - width, None, axis=dim), axis, forward
        )
        high = lax.ppermute(lax.slice_in_dim(block, 0, width, axis=dim), axis, backward)
        block = jnp.concatenate([low, block, high], axis=dim)
    return block


def extend_rows(features):
    row_count = features.shape[1]
    reach_bands = min((PADDING + row_count - 1) // row_count, lax.axis_size("band") - 1)
    upper_blocks = []
    lower_blocks = []
    moving_up = features
    moving_down = features
    for hop_index in range(reach_bands):
        moving_up = from_behind(moving_up, "band", 1)
        moving_down = from_behind(moving_down, "band", -1)
        upper_blocks.insert(0, moving_up)
        lower_blocks.append(moving_down)
    margin = reach_bands * row_count
    stacked = jnp.concatenate(upper_blocks + [features] + lower_blocks, axis=1)
    if margin >= PADDING:
        stacked = stacked[:, margin - PADDING : margin + row_count + PADDING]
    else:
        stacked = jnp.pad(stacked, ((0, 0), (PADDING - margin, PADDING - margin), (0, 0), (0, 0)))
    return jnp.pad(stacked, ((0, 0), (0, 0), (PADDING, PADDING), (0, 0)))


def branch_terms(window, select_rows, weight_one, weight_dilated, live_rows, col_count):
    batches = window.shape[0]
    channels = window.shape[3]
    centre = select_rows(0)[:, :, PADDING : PADDING + col_count].reshape(-1, channels)
    partials = [jnp.dot(centre, weight_one, preferred_element_type=jnp.float32)]
    for branch_index, dilation in enumerate(DILATIONS):
        running = jnp.zeros((centre.shape[0], weight_one.shape[1]), jnp.float32)
        for row_tap in range(3):
            band_rows = select_rows(dilation * (row_tap - 1))
            for col_tap in range(3):
                left = PADDING + dilation * (col_tap - 1)
                tap_rows = band_rows[:, :, left : left + col_count].reshape(-1, channels)
                running = running + jnp.dot(
                    tap_rows,
                    weight_dilated[branch_index, row_tap, col_tap],
                    preferred_element_type=jnp.float32,
                )
        partials.append(running)
    return jnp.concatenate(partials, axis=1).reshape(batches, live_rows, col_count, -1)


def pool_context(features, weight_pool, bias_pool, row_count, col_count):
    local_sum = jnp.sum(features, axis=(1, 2), dtype=jnp.float32)
    cell_count = row_count * lax.axis_size("band") * col_count
    weight_full = weight_pool.astype(jnp.float32)
    average = lax.psum(local_sum, "band") / cell_count
    pre_relu = lax.psum(jnp.dot(average, weight_full, precision=PRECISE), "sect")
    return jax.nn.relu(pre_relu + bias_pool)


def general_shards(
    features,
    low_level,
    land_mask,
    weight_one,
    weight_dilated,
    bias_branch,
    weight_pool,
    bias_pool,
    weight_project,
    bias_project,
    weight_reduce,
    bias_reduce,
    weight_merging,
    bias_merging,
):
    batches, row_count, col_count, channels = features.shape
    branch_width = weight_project.shape[1]
    window = extend_rows(features)
    pooled = pool_context(features, weight_pool, bias_pool, row_count, col_count)
    context = jnp.dot(
        pooled, weight_project[4 * branch_width :].astype(jnp.float32), precision=PRECISE
    )
    row_mask = land_mask.astype(jnp.float32)

    def select_rows(offset):
        return window[:, PADDING + offset : PADDING + offset + row_count]

    partials = branch_terms(window, select_rows, weight_one, weight_dilated, row_count, col_count)
    flat_terms = partials.astype(jnp.bfloat16).reshape(-1, partials.shape[3])
    summed_cells = lax.psum_scatter(flat_terms, "sect", scatter_dimension=0, tiled=True).astype(
        jnp.float32
    )
    share_cells = summed_cells.shape[0]
    first_cell = lax.axis_index("sect") * share_cells
    branch_cells = jax.nn.relu(summed_cells + bias_branch.reshape(-1)).astype(jnp.bfloat16)
    projected_cells = jnp.dot(
        branch_cells, weight_project[: 4 * branch_width], preferred_element_type=jnp.float32
    )
    cell_ids = first_cell + lax.broadcasted_iota(jnp.int32, (share_cells,), 0)
    batch_of = cell_ids // (row_count * col_count)
    batch_onehot = (batch_of[:, None] == lax.broadcasted_iota(jnp.int32, (1, batches), 1)).astype(
        jnp.float32
    )
    context_cells = jnp.dot(batch_onehot, context, precision=PRECISE)
    keep_all = jnp.broadcast_to(row_mask[:, :, None], (batches, row_count, col_count)).reshape(-1)
    keep_cells = lax.dynamic_slice_in_dim(keep_all, first_cell, share_cells, 0)
    out_cells = (
        jax.nn.relu(projected_cells + context_cells + bias_project) * keep_cells[:, None]
    ).astype(jnp.bfloat16)
    project_out = lax.all_gather(out_cells, "sect", axis=0, tiled=True).reshape(
        batches, row_count, col_count, branch_width
    )
    low_reduced = (
        jax.nn.relu(
            jnp.dot(
                low_level.reshape(-1, low_level.shape[3]),
                weight_reduce,
                preferred_element_type=jnp.float32,
            )
            + bias_reduce
        )
        .astype(jnp.bfloat16)
        .reshape(batches, row_count, col_count, -1)
    )
    joined = jnp.concatenate([project_out, low_reduced], axis=3)
    framed = extended(joined, (("band", 1),), 1)
    framed = jnp.pad(framed, ((0, 0), (0, 0), (1, 1), (0, 0)))
    running = jnp.zeros((batches * row_count * col_count, weight_merging.shape[3]), jnp.float32)
    for row_tap in range(3):
        for col_tap in range(3):
            tap_rows = framed[
                :, row_tap : row_tap + row_count, col_tap : col_tap + col_count
            ].reshape(-1, joined.shape[3])
            running = running + jnp.dot(
                tap_rows, weight_merging[row_tap, col_tap], preferred_element_type=jnp.float32
            )
    merged_map = (
        jax.nn.relu(running + bias_merging).reshape(batches, row_count, col_count, -1)
        * row_mask[:, :, None, None]
    )
    return merged_map.astype(jnp.bfloat16)


def solution(mesh):
    in_specs = (
        P("grp", "band", None, "sect"),
        P("grp", "band", None, None),
        P("grp", "band"),
        P("sect", None),
        P(None, None, None, "sect", None),
        P(),
        P("sect", None),
        P(),
        P(),
        P(),
        P(),
        P(),
        P(),
        P(),
    )
    out_specs = P("grp", "band", None, None)

    def chosen(features, low_level, land_mask, weight_one, *others):
        batches, row_count, columns, _ = features.shape
        depths = (low_level.shape[3], weight_one.shape[1])
        sizes = (batches, row_count, columns, mesh.shape["band"], mesh.shape["sect"])
        body = shards if fits(*sizes, *depths) else general_shards
        return body(features, low_level, land_mask, weight_one, *others)

    return jax.shard_map(
        chosen, mesh=mesh, in_specs=in_specs, out_specs=out_specs, check_vma=False
    )
```

```python
import functools

import jax
import jax.numpy as jnp
from jax import lax
from jax.experimental import pallas as pl
from jax.experimental.pallas import tpu as pltpu
from jax.sharding import PartitionSpec as P

DILATIONS = (12, 24, 36)
PADDING = 36
PRECISE = lax.Precision.HIGHEST
ROW_BLOCK = 6
MOST_LAND = 4
VMEM_LIMIT = 32 * 2 ** 20
WHOLE_VMEM = 58 * 2 ** 20
POOL_ROWS = 8
F32 = jnp.float32
BF16 = jnp.bfloat16
VMEM = pl.BlockSpec(memory_space=pltpu.VMEM)
HBM = pl.BlockSpec(memory_space=pltpu.HBM)


def call(body, outs, in_specs, scratch, limit=VMEM_LIMIT):
    return pl.pallas_call(
        body,
        out_shape=outs,
        in_specs=in_specs,
        out_specs=jax.tree.map(lambda _: VMEM, outs),
        scratch_shapes=scratch,
        compiler_params=pltpu.CompilerParams(vmem_limit_bytes=limit),
        cost_estimate=pl.CostEstimate(flops=1024, bytes_accessed=1024, transcendentals=0),
    )


def reversed_bits(value, bits):
    return sum(((value >> bit) & 1) << (bits - 1 - bit) for bit in range(bits))


def fill_slots(mask_ref, slots_ref, batches, row_count):
    for image in range(batches):
        inner = range(1, row_count - 1)
        lives = {row: (mask_ref[image, row] > 0).astype(jnp.int32) for row in inner}
        land_total = sum(lives.values())
        land_before, sea_before = 0, 0
        chosen = [0] * (MOST_LAND - 2)
        for row in inner:
            live = lives[row]
            rank = jnp.where(live > 0, land_before, land_total + sea_before)
            chosen = [
                value + row * (rank == slot).astype(jnp.int32)
                for slot, value in enumerate(chosen)
            ]
            land_before = land_before + live
            sea_before = sea_before + (1 - live)
        base = image * MOST_LAND
        rows = [jnp.int32(0), *chosen, jnp.int32(row_count - 1)]
        flags = [(land_total > slot).astype(jnp.int32) for slot in range(MOST_LAND - 2)]
        flags = [mask_ref[image, 0], *flags, mask_ref[image, row_count - 1]]
        for slot in range(MOST_LAND):
            slots_ref[0, base + slot] = rows[slot]
            slots_ref[1, base + slot] = flags[slot]


def split_three(value):
    high = value.astype(BF16)
    rest = value - high.astype(F32)
    middle = rest.astype(BF16)
    low = (rest - middle.astype(F32)).astype(BF16)
    return high, middle, low


def precise_dot(value, weight):
    return sum(jnp.dot(part, weight, preferred_element_type=F32) for part in split_three(value))


def shifted(value, by, columns):
    blocks = value.reshape(-1, columns, value.shape[1])
    empty = jnp.zeros((blocks.shape[0], abs(by), value.shape[1]), value.dtype)
    if by > 0:
        moved = jnp.concatenate([empty, blocks[:, : columns - by]], axis=1)
    else:
        moved = jnp.concatenate([blocks[:, -by:], empty], axis=1)
    return moved.reshape(value.shape)


class Plan:
    def __init__(self, batches, row_count, columns, bands, sects):
        self.batches, self.row_count, self.columns = batches, row_count, columns
        self.bands, self.sects = bands, sects
        self.bits = sects.bit_length() - 1
        self.share_rows = batches * MOST_LAND // sects
        self.share = self.share_rows * columns
        self.terms = []
        for branch, dilation in enumerate(DILATIONS):
            hop = dilation // row_count
            if hop >= bands:
                continue
            up = [(b, b + hop) for b in range(bands - hop)]
            down = [(target, source) for source, target in up]
            if 2 * hop >= bands:
                self.terms.append((branch, hop, None, up + down))
            else:
                self.terms.append((branch, hop, 0, up))
                self.terms.append((branch, hop, 2, down))

    def rows_of(self, position, sect, slots_ref):
        owner = sect ^ reversed_bits(position, self.bits)
        for row in range(self.share_rows):
            place = owner * self.share_rows + row
            start = (position * self.share_rows + row) * self.columns
            yield lax.div(place, MOST_LAND), slots_ref[0, place], start


def tap_sum(rows, taps, dilation, columns):
    width = taps.shape[1] // 3
    if dilation >= columns:
        return jnp.dot(rows, taps[:, width : 2 * width], preferred_element_type=F32)
    channels = rows.shape[1]
    image = rows.reshape(-1, columns, channels)
    reach = columns - dilation // 16 * 16
    first = jnp.dot(image[:, :reach].reshape(-1, channels), taps[:, :width], preferred_element_type=F32)
    last = jnp.dot(image[:, columns - reach :].reshape(-1, channels), taps[:, 2 * width :], preferred_element_type=F32)
    middle = jnp.dot(rows, taps[:, width : 2 * width], preferred_element_type=F32).reshape(-1, columns, width)
    first = first.reshape(-1, reach, width)[:, : columns - dilation]
    last = last.reshape(-1, reach, width)[:, reach - (columns - dilation) :]
    gap = jnp.zeros((first.shape[0], dilation, width), F32)
    total = middle + jnp.concatenate([gap, first], axis=1) + jnp.concatenate([last, gap], axis=1)
    return total.reshape(-1, width)


def store_halves(keep, send, index, value):
    half, width = keep.shape[0], value.shape[1]
    value = value.astype(BF16)
    keep[:, pl.ds(index * width, width)] = value[:half]
    send[:, pl.ds(index * width, width)] = value[half:]


def gather(plan, mask, features_ref, slots_ref, rows_ref):
    fill_slots(mask, slots_ref, plan.batches, plan.row_count)
    sect = lax.axis_index("sect")
    for position in range(plan.sects):
        for image, row, start in plan.rows_of(position, sect, slots_ref):
            rows_ref[pl.ds(start, plan.columns)] = features_ref[image, row]


def parts_of(value):
    high, low, _ = split_three(value)
    return jnp.concatenate([high.astype(F32), low.astype(F32)], axis=0)


def joined_parts(rows):
    return rows[:POOL_ROWS].astype(F32) + rows[POOL_ROWS:].astype(F32)


def pool_kernel(features_ref, weight_ref, out_ref):
    batches, row_count, columns, channels = features_ref.shape
    row = lax.broadcasted_iota(jnp.int32, (POOL_ROWS, channels), 0)
    sums = jnp.zeros((POOL_ROWS, channels), F32)
    for image in range(batches):
        cells = features_ref[image].astype(F32).reshape(row_count * columns, channels)
        sums = jnp.where(row == image, jnp.sum(cells, axis=0, keepdims=True), sums)
    out_ref[...] = parts_of(precise_dot(sums, weight_ref[...])).astype(BF16)


def copy_edges(plan, low_ref, out_ref, parity):
    upper = lax.rem(lax.axis_index("band") + parity, 2) == 0
    row = jnp.where(upper, plan.row_count - 1, 0)
    for image in range(plan.batches):
        out_ref[pl.ds(image * plan.columns, plan.columns)] = low_ref[image, row]


def second_edge_kernel(plan, low_ref, out_ref):
    copy_edges(plan, low_ref, out_ref, 1)


def edge_kernel(plan, low_ref, keep_ref, moved_ref, far_ref, first_ref):
    far = keep_ref[...].astype(F32) + moved_ref[...].astype(F32)
    far_ref[...] = far.astype(BF16)
    cells, width = plan.batches * plan.columns, low_ref.shape[3]
    first_ref[pl.ds(cells, 2 * POOL_ROWS)] = far[plan.share :, :width].astype(BF16)
    copy_edges(plan, low_ref, first_ref, 0)


def fetch_taps(dilated_ref, branch, row_tap, taps_ref, index, sems):
    width = dilated_ref.shape[4]
    copies = []
    for tap in range(3):
        copy = pltpu.make_async_copy(
            dilated_ref.at[branch, row_tap, tap],
            taps_ref.at[index, :, pl.ds(tap * width, width)],
            sems.at[index, tap],
        )
        copy.start()
        copies.append(copy)
    return copies


def own_kernel(plan, mask_ref, features_ref, one_ref, dilated_ref, keep, send, *refs):
    terms = len(plan.terms)
    far_taps, refs = refs[:terms], refs[terms:]
    slots_ref, land_ref, held_ref, rows_ref, ones_ref, taps_ref, sems, tap_sems, far_sems = refs
    copies = [
        pltpu.make_async_copy(mask_ref, land_ref, sems.at[0]),
        pltpu.make_async_copy(features_ref, held_ref, sems.at[1]),
        pltpu.make_async_copy(one_ref, ones_ref, sems.at[2]),
    ]
    for copy in copies:
        copy.start()
    tap_copies = [fetch_taps(dilated_ref, 0, 1, taps_ref, 0, tap_sems)]
    copies[0].wait()
    copies[1].wait()
    for branch in range(1, len(DILATIONS)):
        tap_copies.append(fetch_taps(dilated_ref, branch, 1, taps_ref, branch, tap_sems))
    gather(plan, land_ref, held_ref, slots_ref, rows_ref)
    far_copies = []
    for term, (branch, hop, row_tap, _) in enumerate(plan.terms):
        if row_tap is None:
            row_tap = jnp.where(lax.axis_index("band") + hop < plan.bands, 0, 2)
        far_copies.append(
            pltpu.make_async_copy(dilated_ref.at[branch, row_tap], far_taps[term], far_sems.at[term])
        )
        far_copies[-1].start()
    copies[2].wait()
    value = jnp.dot(rows_ref[...], ones_ref[...], preferred_element_type=F32)
    store_halves(keep, send, 0, value)
    for branch, waits in enumerate(tap_copies):
        for copy in waits:
            copy.wait()
        half = keep.shape[0]
        width = taps_ref.shape[2] // 3
        lanes = pl.ds((branch + 1) * width, width)
        for out, start in ((send, half), (keep, 0)):
            value = tap_sum(rows_ref[pl.ds(start, half)], taps_ref[branch], DILATIONS[branch], plan.columns)
            out[:, lanes] = value.astype(BF16)
    for copy in far_copies:
        copy.wait()


def own_partials(plan, mask, features, weight_one, weight_dilated):
    channels, width = weight_one.shape
    half = plan.sects // 2 * plan.share
    out = jax.ShapeDtypeStruct((half, (1 + len(DILATIONS)) * width), BF16)
    return call(
        functools.partial(own_kernel, plan),
        (out, out, *[jax.ShapeDtypeStruct((3, channels, width), BF16) for _ in plan.terms]),
        [HBM, HBM, HBM, HBM],
        [
            pltpu.SMEM((2, plan.batches * MOST_LAND), jnp.int32),
            pltpu.SMEM(mask.shape, jnp.int32),
            pltpu.VMEM(features.shape, BF16),
            pltpu.VMEM((2 * half, channels), BF16),
            pltpu.VMEM((channels, width), BF16),
            pltpu.VMEM((len(DILATIONS), channels, 3 * width), BF16),
            pltpu.SemaphoreType.DMA((3,)),
            pltpu.SemaphoreType.DMA((len(DILATIONS), 3)),
            pltpu.SemaphoreType.DMA((len(plan.terms),)),
        ],
        WHOLE_VMEM,
    )(mask, features, weight_one, weight_dilated)


def far_kernel(plan, far_mask_ref, pool_ref, features_ref, *refs):
    terms = len(plan.terms)
    taps_refs, (keep, send, slots_ref, rows_ref) = refs[:terms], refs[terms:]
    pooled = pool_ref[...]
    block = plan.share + 2 * POOL_ROWS
    for term, taps_ref in enumerate(taps_refs):
        width = taps_ref.shape[2]
        gather(plan, far_mask_ref.at[term], features_ref, slots_ref, rows_ref)
        taps = jnp.concatenate([taps_ref[tap] for tap in range(3)], axis=1)
        dilation = DILATIONS[plan.terms[term][0]]
        value = tap_sum(rows_ref[...], taps, dilation, plan.columns).astype(BF16)
        lanes = pl.ds(term * width, width)
        for position in range(plan.sects):
            out = keep if position < plan.sects // 2 else send
            start = position % (plan.sects // 2) * block
            share = value[position * plan.share : (position + 1) * plan.share]
            out[pl.ds(start, plan.share), lanes] = share
            out[pl.ds(start + plan.share, 2 * POOL_ROWS), lanes] = pooled


def far_partials(plan, far_mask, pool, features, taps):
    channels, width = taps[0].shape[1:]
    rows = plan.sects // 2 * (plan.share + 2 * POOL_ROWS)
    out = jax.ShapeDtypeStruct((rows, len(taps) * width), BF16)
    return call(
        functools.partial(far_kernel, plan),
        (out, out),
        [VMEM] * (3 + len(taps)),
        [
            pltpu.SMEM((2, plan.batches * MOST_LAND), jnp.int32),
            pltpu.VMEM((plan.sects * plan.share, channels), BF16),
        ],
    )(far_mask, pool, features, *taps)


def low_kernel(plan, low_ref, first_ref, second_ref, reduce_ref, bias_reduce_ref, merging_ref, bias_ref, out_ref, framed_ref):
    batches, row_count, columns, depth = low_ref.shape
    band, bands = lax.axis_index("band"), plan.bands
    reduced = reduce_ref.shape[1]
    wide = 3 * reduced
    even = lax.rem(band, 2) == 0
    copied = lax.broadcasted_iota(jnp.int32, (reduced, wide), 1) % reduced
    copies = (copied == lax.broadcasted_iota(jnp.int32, (reduced, wide), 0)).astype(F32).astype(BF16)
    weight = jnp.dot(reduce_ref[...], copies, preferred_element_type=F32).astype(BF16)
    bias = precise_dot(bias_reduce_ref[...], copies)

    def reduce(rows):
        value = jnp.dot(rows, weight, preferred_element_type=F32) + bias
        value = jnp.maximum(value, 0.0).astype(BF16).astype(F32)
        lane = lax.broadcasted_iota(jnp.int32, value.shape, 1)
        return jnp.where(
            lane < reduced,
            shifted(value, 1, columns),
            jnp.where(lane < 2 * reduced, value, shifted(value, -1, columns)),
        )

    framed_ref[:, 1 : row_count + 1] = (
        reduce(low_ref[...].reshape(-1, depth)).astype(BF16).reshape(batches, row_count, columns, wide)
    )
    first = reduce(first_ref[: batches * columns])
    second = reduce(second_ref[...])
    above = jnp.where(even, second, first) * jnp.where(band > 0, 1.0, 0.0)
    below = jnp.where(even, first, second) * jnp.where(band < bands - 1, 1.0, 0.0)
    framed_ref[:, 0] = above.astype(BF16).reshape(batches, columns, wide)
    framed_ref[:, row_count + 1] = below.astype(BF16).reshape(batches, columns, wide)
    width = merging_ref.shape[2] - reduced
    for image in range(batches):
        total = jnp.zeros((row_count * columns, out_ref.shape[3]), F32) + bias_ref[...]
        for tap in range(3):
            rows = framed_ref[image, tap : tap + row_count].reshape(-1, wide)
            taps = jnp.concatenate([merging_ref[tap, side, width:] for side in range(3)], axis=0)
            total = total + jnp.dot(rows, taps, preferred_element_type=F32)
        out_ref[image] = total.reshape(row_count, columns, -1)


def project_kernel(plan, mask_ref, keep_ref, moved_ref, bias_branch_ref, pool_ref, bias_pool_ref, weight_ref, bias_ref, *refs):
    far_refs = refs[: len(plan.terms)]
    out_ref, edge_ref, slots_ref, context_ref = refs[len(plan.terms) :]
    columns, width = plan.columns, weight_ref.shape[1]
    sect = lax.axis_index("sect")
    fill_slots(mask_ref, slots_ref, plan.batches, plan.row_count)
    cells = plan.row_count * plan.bands * columns
    pooled = pool_ref[...] / cells
    pooled = jnp.maximum(pooled + bias_pool_ref[...], 0.0)
    context_ref[...] = precise_dot(pooled, weight_ref[4 * width :]) + bias_ref[...]
    total = jnp.zeros((plan.share, width), F32)
    for branch in range(4):
        lanes = pl.ds(branch * width, width)
        value = keep_ref[:, lanes].astype(F32) + moved_ref[:, lanes].astype(F32)
        for term, far in zip(plan.terms, far_refs):
            if term[0] + 1 == branch:
                value = value + far[: plan.share].astype(F32)
        value = jnp.maximum(value + bias_branch_ref[pl.ds(branch, 1)], 0.0).astype(BF16)
        total = total + jnp.dot(
            value, weight_ref[pl.ds(branch * width, width)], preferred_element_type=F32
        )
    for row in range(plan.share_rows):
        place = sect * plan.share_rows + row
        image = lax.div(place, MOST_LAND)
        keep = slots_ref[1, place].astype(F32)
        value = total[row * columns : (row + 1) * columns] + context_ref[pl.ds(image, 1)]
        out_ref[pl.ds(row * columns, columns)] = (jnp.maximum(value, 0.0) * keep).astype(BF16)
    at_top = lax.rem(sect * plan.share_rows, MOST_LAND) == 0

    @pl.when(at_top)
    def _():
        edge_ref[...] = out_ref[pl.ds(0, columns)]

    @pl.when(jnp.logical_not(at_top))
    def _():
        edge_ref[...] = out_ref[pl.ds(plan.share - columns, columns)]


def merge_kernel(plan, mask_ref, low_ref, weight_ref, *refs):
    sects, columns = plan.sects, plan.columns
    share_refs, edge_refs = refs[:sects], refs[sects : 2 * sects]
    out_ref, slots_ref, rows_ref, halo_ref, total_ref = refs[2 * sects :]
    width = weight_ref.shape[3]
    sect = lax.axis_index("sect")
    fill_slots(mask_ref, slots_ref, plan.batches, plan.row_count)

    def spread(value):
        wide = value.astype(F32)
        return (
            shifted(wide, 1, columns).astype(BF16),
            value,
            shifted(wide, -1, columns).astype(BF16),
        )

    def weight(tap):
        return jnp.concatenate([weight_ref[tap, side, :width] for side in range(3)], axis=0)

    total_ref[:, 1 : plan.row_count + 1] = low_ref[...]
    tops, bottoms = [], []
    for offset in range(sects):
        for side, value in enumerate(spread(share_refs[offset][...])):
            rows_ref[pl.ds(offset * plan.share, plan.share), pl.ds(side * width, width)] = value
        for side, value in enumerate(spread(edge_refs[offset][...])):
            halo_ref[pl.ds(offset * columns, columns), pl.ds(side * width, width)] = value
    for tap in range(3):
        taps = weight(tap)
        result = jnp.dot(rows_ref[...], taps, preferred_element_type=F32)
        if tap != 1:
            halo = jnp.dot(halo_ref[...], taps, preferred_element_type=F32)
        for offset in range(sects):
            owner = sect ^ offset
            for row in range(plan.share_rows):
                place = owner * plan.share_rows + row
                image = lax.div(place, MOST_LAND)
                at = slots_ref[0, place] + 2 - tap
                start = (offset * plan.share_rows + row) * columns
                total_ref[image, at] = total_ref[image, at] + result[start : start + columns]
            first = owner * plan.share_rows
            image = lax.div(first, MOST_LAND)
            top = lax.rem(first, MOST_LAND) == 0
            bottom = lax.rem(first + plan.share_rows, MOST_LAND) == 0
            if tap != 1:
                piece = halo[offset * columns : (offset + 1) * columns]
                at = 1 if tap == 0 else plan.row_count
                factor = jnp.where(top if tap == 0 else bottom, 1.0, 0.0)
                total_ref[image, at] = total_ref[image, at] + piece * factor
    for image in range(plan.batches):
        for row in range(plan.row_count):
            keep = mask_ref[image, row].astype(F32)
            out_ref[image, row] = (jnp.maximum(total_ref[image, row + 1], 0.0) * keep).astype(BF16)


def swap(value, axis, pattern):
    count = lax.axis_size(axis)
    return lax.ppermute(value, axis, [(i, i ^ pattern) for i in range(count)])


def add_halves(keep, moved):
    half = keep.shape[0] // 2
    return tuple(
        (keep[rows].astype(F32) + moved[rows].astype(F32)).astype(BF16)
        for rows in (slice(0, half), slice(half, 2 * half))
    )


def spread_over(value, plan):
    values = {0: value}
    for bit in reversed(range(plan.bits)):
        for offset in list(values):
            values[offset ^ 1 << bit] = swap(values[offset], "sect", 1 << bit)
    return [values[offset] for offset in range(plan.sects)]


def swap_edges(edge, plan):
    pairs = []
    for image in range(plan.batches):
        top = image * MOST_LAND // plan.share_rows
        bottom = (image * MOST_LAND + MOST_LAND - 1) // plan.share_rows
        for band in range(plan.bands - 1):
            upper = band * plan.sects + bottom
            lower = (band + 1) * plan.sects + top
            pairs += [(upper, lower), (lower, upper)]
    return lax.ppermute(edge, ("band", "sect"), pairs)


def border_pairs(bands):
    pairs = []
    for band in range(1, bands - 1, 2):
        pairs += [(band, band + 1), (band + 1, band)]
    return pairs


def fits(batches, row_count, columns, bands, sects, low_depth, width):
    slots = batches * MOST_LAND
    return (
        row_count == ROW_BLOCK
        and all(dilation % row_count == 0 for dilation in DILATIONS)
        and sects > 1
        and sects & (sects - 1) == 0
        and bands > min(DILATIONS) // row_count
        and low_depth == width
        and bands & (bands - 1) == 0
        and slots % sects == 0
        and MOST_LAND % (2 * (slots // sects)) == 0
        and columns % 16 == 0
        and batches <= POOL_ROWS
    )


def shards(
    features,
    low_level,
    land_mask,
    weight_one,
    weight_dilated,
    bias_branch,
    weight_pool,
    bias_pool,
    weight_project,
    bias_project,
    weight_reduce,
    bias_reduce,
    weight_merging,
    bias_merging,
):
    batches, row_count, columns, channels = features.shape
    bands, sects = lax.axis_size("band"), lax.axis_size("sect")
    plan = Plan(batches, row_count, columns, bands, sects)
    width = weight_one.shape[1]
    band = lax.axis_index("band")
    keep, send, *taps = own_partials(plan, land_mask, features, weight_one, weight_dilated)
    keep, send, late_mask, late_features, late_low = lax.optimization_barrier(
        (keep, send, land_mask, features, low_level)
    )
    far_masks = [
        lax.ppermute(late_mask, "band", [(target, source) for source, target in pairs])
        for _, _, _, pairs in plan.terms
    ]
    pool = call(
        pool_kernel, jax.ShapeDtypeStruct((2 * POOL_ROWS, width), BF16), [VMEM, VMEM], []
    )(late_features, weight_pool)
    moved = swap(send, "sect", 1)
    for bit in range(1, plan.bits - 1):
        keep, send = add_halves(keep, moved)
        moved = swap(send, "sect", 1 << bit)
    keep, send = add_halves(keep, moved)
    moved = swap(send, "sect", plan.sects // 2)
    far_mask = jnp.stack(far_masks)
    far_mask, send = lax.optimization_barrier((far_mask, send))
    far_keep, far_send = far_partials(plan, far_mask, pool, late_features, taps)
    far_keep, far_send, late_low = lax.optimization_barrier((far_keep, far_send, late_low))
    for bit in range(plan.bits - 1):
        far_moved = swap(far_send, "sect", 1 << bit)
        far_keep, far_send = add_halves(far_keep, far_moved)
    far_moved = swap(far_send, "sect", plan.sects // 2)
    second = call(
        functools.partial(second_edge_kernel, plan),
        jax.ShapeDtypeStruct((batches * columns, width), BF16),
        [VMEM],
        [],
    )(late_low)
    second = lax.ppermute(second, "band", border_pairs(bands))
    far_moved, second = lax.optimization_barrier((far_moved, second))
    far, first = call(
        functools.partial(edge_kernel, plan),
        (
            jax.ShapeDtypeStruct(far_keep.shape, BF16),
            jax.ShapeDtypeStruct((batches * columns + 2 * POOL_ROWS, width), BF16),
        ),
        [VMEM] * 3,
        [],
    )(late_low, far_keep, far_moved)
    far_terms = []
    for term, (_, hop, _, pairs) in enumerate(plan.terms):
        rows = far if 2 * hop == bands else far[: plan.share]
        lanes = slice(term * width, (term + 1) * width)
        far_terms.append(lax.ppermute(rows[:, lanes], "band", pairs))
    own_pool = far[plan.share :, :width]
    first = swap(first, "band", 1)
    pool = joined_parts(own_pool) + joined_parts(first[batches * columns :])
    if bands == 4 and any(2 * term[1] == bands for term in plan.terms):
        halves = [term for term, entry in enumerate(plan.terms) if 2 * entry[1] == bands]
        pool = pool + joined_parts(far_terms[halves[0]][plan.share :])
        pool = pool + joined_parts(swap(own_pool, "band", 3))
    else:
        for bit in range(1, bands.bit_length() - 1):
            pool = pool + swap(pool, "band", 1 << bit)
    reduced = weight_reduce.shape[1]
    low_part = call(
        functools.partial(low_kernel, plan),
        jax.ShapeDtypeStruct((batches, row_count, columns, weight_merging.shape[3]), F32),
        [VMEM] * 7,
        [pltpu.VMEM((batches, row_count + 2, columns, 3 * reduced), BF16)],
    )(
        late_low,
        first,
        second,
        weight_reduce,
        bias_reduce[None],
        weight_merging,
        bias_merging[None],
    )
    keep, low_part = lax.optimization_barrier((keep, low_part))
    share = jax.ShapeDtypeStruct((plan.share, width), BF16)
    row = jax.ShapeDtypeStruct((columns, width), BF16)
    out, edge = call(
        functools.partial(project_kernel, plan),
        (share, row),
        [VMEM] * (8 + len(plan.terms)),
        [pltpu.SMEM((2, batches * MOST_LAND), jnp.int32), pltpu.VMEM((8, width), F32)],
    )(
        land_mask,
        keep,
        moved,
        bias_branch,
        pool,
        bias_pool[None],
        weight_project,
        bias_project[None],
        *far_terms,
    )
    halo = swap_edges(edge, plan)
    shares, halos = spread_over(out, plan), spread_over(halo, plan)
    live = batches * MOST_LAND * columns
    return call(
        functools.partial(merge_kernel, plan),
        jax.ShapeDtypeStruct(low_part.shape, BF16),
        [VMEM] * (3 + 2 * sects),
        [
            pltpu.SMEM((2, batches * MOST_LAND), jnp.int32),
            pltpu.VMEM((live, 3 * width), BF16),
            pltpu.VMEM((sects * columns, 3 * width), BF16),
            pltpu.VMEM((batches, row_count + 2, columns, width), F32),
        ],
    )(land_mask, low_part, weight_merging, *shares, *halos)


def from_behind(value, axis, by):
    count = lax.axis_size(axis)
    pairs = [(i, i + by) for i in range(count) if 0 <= i + by < count]
    return lax.ppermute(value, axis, pairs)


def extended(block, sides, width):
    for axis, dim in sides:
        count = lax.axis_size(axis)
        forward = [(i, i + 1) for i in range(count - 1)]
        backward = [(target, source) for source, target in forward]
        low = lax.ppermute(
            lax.slice_in_dim(block, block.shape[dim] - width, None, axis=dim), axis, forward
        )
        high = lax.ppermute(lax.slice_in_dim(block, 0, width, axis=dim), axis, backward)
        block = jnp.concatenate([low, block, high], axis=dim)
    return block


def extend_rows(features):
    row_count = features.shape[1]
    reach_bands = min((PADDING + row_count - 1) // row_count, lax.axis_size("band") - 1)
    upper_blocks = []
    lower_blocks = []
    moving_up = features
    moving_down = features
    for hop_index in range(reach_bands):
        moving_up = from_behind(moving_up, "band", 1)
        moving_down = from_behind(moving_down, "band", -1)
        upper_blocks.insert(0, moving_up)
        lower_blocks.append(moving_down)
    margin = reach_bands * row_count
    stacked = jnp.concatenate(upper_blocks + [features] + lower_blocks, axis=1)
    if margin >= PADDING:
        stacked = stacked[:, margin - PADDING : margin + row_count + PADDING]
    else:
        stacked = jnp.pad(stacked, ((0, 0), (PADDING - margin, PADDING - margin), (0, 0), (0, 0)))
    return jnp.pad(stacked, ((0, 0), (0, 0), (PADDING, PADDING), (0, 0)))


def branch_terms(window, select_rows, weight_one, weight_dilated, live_rows, col_count):
    batches = window.shape[0]
    channels = window.shape[3]
    centre = select_rows(0)[:, :, PADDING : PADDING + col_count].reshape(-1, channels)
    partials = [jnp.dot(centre, weight_one, preferred_element_type=jnp.float32)]
    for branch_index, dilation in enumerate(DILATIONS):
        running = jnp.zeros((centre.shape[0], weight_one.shape[1]), jnp.float32)
        for row_tap in range(3):
            band_rows = select_rows(dilation * (row_tap - 1))
            for col_tap in range(3):
                left = PADDING + dilation * (col_tap - 1)
                tap_rows = band_rows[:, :, left : left + col_count].reshape(-1, channels)
                running = running + jnp.dot(
                    tap_rows,
                    weight_dilated[branch_index, row_tap, col_tap],
                    preferred_element_type=jnp.float32,
                )
        partials.append(running)
    return jnp.concatenate(partials, axis=1).reshape(batches, live_rows, col_count, -1)


def pool_context(features, weight_pool, bias_pool, row_count, col_count):
    local_sum = jnp.sum(features, axis=(1, 2), dtype=jnp.float32)
    cell_count = row_count * lax.axis_size("band") * col_count
    weight_full = weight_pool.astype(jnp.float32)
    average = lax.psum(local_sum, "band") / cell_count
    pre_relu = lax.psum(jnp.dot(average, weight_full, precision=PRECISE), "sect")
    return jax.nn.relu(pre_relu + bias_pool)


def general_shards(
    features,
    low_level,
    land_mask,
    weight_one,
    weight_dilated,
    bias_branch,
    weight_pool,
    bias_pool,
    weight_project,
    bias_project,
    weight_reduce,
    bias_reduce,
    weight_merging,
    bias_merging,
):
    batches, row_count, col_count, channels = features.shape
    branch_width = weight_project.shape[1]
    window = extend_rows(features)
    pooled = pool_context(features, weight_pool, bias_pool, row_count, col_count)
    context = jnp.dot(
        pooled, weight_project[4 * branch_width :].astype(jnp.float32), precision=PRECISE
    )
    row_mask = land_mask.astype(jnp.float32)

    def select_rows(offset):
        return window[:, PADDING + offset : PADDING + offset + row_count]

    partials = branch_terms(window, select_rows, weight_one, weight_dilated, row_count, col_count)
    flat_terms = partials.astype(jnp.bfloat16).reshape(-1, partials.shape[3])
    summed_cells = lax.psum_scatter(flat_terms, "sect", scatter_dimension=0, tiled=True).astype(
        jnp.float32
    )
    share_cells = summed_cells.shape[0]
    first_cell = lax.axis_index("sect") * share_cells
    branch_cells = jax.nn.relu(summed_cells + bias_branch.reshape(-1)).astype(jnp.bfloat16)
    projected_cells = jnp.dot(
        branch_cells, weight_project[: 4 * branch_width], preferred_element_type=jnp.float32
    )
    cell_ids = first_cell + lax.broadcasted_iota(jnp.int32, (share_cells,), 0)
    batch_of = cell_ids // (row_count * col_count)
    batch_onehot = (batch_of[:, None] == lax.broadcasted_iota(jnp.int32, (1, batches), 1)).astype(
        jnp.float32
    )
    context_cells = jnp.dot(batch_onehot, context, precision=PRECISE)
    keep_all = jnp.broadcast_to(row_mask[:, :, None], (batches, row_count, col_count)).reshape(-1)
    keep_cells = lax.dynamic_slice_in_dim(keep_all, first_cell, share_cells, 0)
    out_cells = (
        jax.nn.relu(projected_cells + context_cells + bias_project) * keep_cells[:, None]
    ).astype(jnp.bfloat16)
    project_out = lax.all_gather(out_cells, "sect", axis=0, tiled=True).reshape(
        batches, row_count, col_count, branch_width
    )
    low_reduced = (
        jax.nn.relu(
            jnp.dot(
                low_level.reshape(-1, low_level.shape[3]),
                weight_reduce,
                preferred_element_type=jnp.float32,
            )
            + bias_reduce
        )
        .astype(jnp.bfloat16)
        .reshape(batches, row_count, col_count, -1)
    )
    joined = jnp.concatenate([project_out, low_reduced], axis=3)
    framed = extended(joined, (("band", 1),), 1)
    framed = jnp.pad(framed, ((0, 0), (0, 0), (1, 1), (0, 0)))
    running = jnp.zeros((batches * row_count * col_count, weight_merging.shape[3]), jnp.float32)
    for row_tap in range(3):
        for col_tap in range(3):
            tap_rows = framed[
                :, row_tap : row_tap + row_count, col_tap : col_tap + col_count
            ].reshape(-1, joined.shape[3])
            running = running + jnp.dot(
                tap_rows, weight_merging[row_tap, col_tap], preferred_element_type=jnp.float32
            )
    merged_map = (
        jax.nn.relu(running + bias_merging).reshape(batches, row_count, col_count, -1)
        * row_mask[:, :, None, None]
    )
    return merged_map.astype(jnp.bfloat16)


def solution(mesh):
    in_specs = (
        P("grp", "band", None, "sect"),
        P("grp", "band", None, None),
        P("grp", "band"),
        P("sect", None),
        P(None, None, None, "sect", None),
        P(),
        P("sect", None),
        P(),
        P(),
        P(),
        P(),
        P(),
        P(),
        P(),
    )
    out_specs = P("grp", "band", None, None)

    def chosen(features, low_level, land_mask, weight_one, *others):
        batches, row_count, columns, _ = features.shape
        depths = (low_level.shape[3], weight_one.shape[1])
        sizes = (batches, row_count, columns, mesh.shape["band"], mesh.shape["sect"])
        body = shards if fits(*sizes, *depths) else general_shards
        return body(features, low_level, land_mask, weight_one, *others)

    return jax.shard_map(
        chosen, mesh=mesh, in_specs=in_specs, out_specs=out_specs, check_vma=False
    )
```
